512 devices in a mesh: query: 16 (over z, core), passage: 32 (over y, x).
Axes of the slice: x: 4, y: 8, z: 8, core: 2. Of those that a mesh axis runs over, the one named last changes fastest.
Arguments:
- query_tokens: bfloat16 [512, 32, 128], P(('query', 'passage')), may hold values from -3 to 3
- passage_tokens: bfloat16 [2048, 128, 128], P('passage'), may hold values from -3 to 3
- passage_lengths: int32 [2048], replicated, may hold values from 32 to 128
- cand_shard: int32 [512, 256, 1], P('query'), may hold values from 0 to 31; in each aligned block of 8192 rows (0 to 8191, 8192 to 16383, ..., all dimensions but the last counted through in order) at most 512 rows name the same one
- cand_local: int32 [512, 256], P('query'), may hold values from 0 to 63
- teacher_scores: float32 [512, 256], P('query'), may hold values from -20 to 320
Outputs:
- loss: float32 [], replicated
- query_grads: float32 [512, 32, 128], P(('query', 'passage'))
The draws below stay inside these ranges and needn't reach their ends.
Inputs may be any that keep to these rules, and one draw needn't show every extreme that they name: `cand_shard`: within one group's list (aligned blocks of 8192 entries), no shard is named more than 512 times; in some group some shard is named exactly 512 times.
All inputs are finite; a program needn't handle non-finite values.
Results may differ from the reference program's by a relative error of at most 0.003.
Values may be sent and summed in bfloat16 or wider, within the bound.
No kernel may reach another device: no remote copies, remote signals or barrier semaphores. Data moves between devices by JAX's collectives and lax.ppermute only.
A program may use at most 64 MiB of HBM per device.

```python
import math
import jax
import jax.numpy as jnp
import numpy as np
from jax import lax

DIM = 128
QLEN = 32
PLEN = 128
CAND = 256
PASS_DEV = 64
SHARDS = 32
QRY_GRP = 32
QUERIES = 512
PASSAGES = 2048
MOST = 512


def draw_query_tokens(key, part):
    base_scale = DIM ** (-0.25)
    entries = jnp.clip(jax.random.normal(key, (QUERIES, QLEN, DIM), jnp.float32) * base_scale, -3.0, 3.0)
    return entries.astype(jnp.bfloat16)


def draw_passage_tokens(key, part):
    base_scale = DIM ** (-0.25)
    entries = jnp.clip(jax.random.normal(key, (PASSAGES, PLEN, DIM), jnp.float32) * base_scale, -3.0, 3.0)
    return entries.astype(jnp.bfloat16)


def draw_teacher_scores(key, part):
    ramp = 3.0 ** (jnp.arange(QUERIES).astype(jnp.float32) / max(QUERIES - 1, 1))
    entries = jnp.clip(jax.random.normal(key, (QUERIES, CAND), jnp.float32) * 2.0 * ramp[:, None], -20.0, 20.0)
    return entries.astype(jnp.float32)


def plant(result, stream_key, low, top_value):
    extent = result.shape
    place = [jax.random.randint(jax.random.fold_in(stream_key, axis), (), 0, extent[axis]) for axis in range(len(extent))]
    result = result.at[tuple(place)].set(low)
    longest = extent.index(max(extent))
    place[longest] = (place[longest] + 1) % extent[longest]
    return result.at[tuple(place)].set(top_value)


def deal_out(key, own, number, rows, amount, top, limit, skew):
    ranking = jax.random.permutation(key, amount)
    packed, common = shares(amount, rows * top, limit, skew, True), shares(amount, rows * top, limit, skew, False)
    places = jnp.arange(amount)

    def named(lengths, rotation):
        used = int((lengths > 0).sum())
        fixed = max(1, used // 4)
        passed = fixed + (places - fixed + rotation * (used - fixed)) % max(1, amount - fixed)
        return jnp.zeros((amount,), jnp.int32).at[ranking[jnp.where(places < fixed, places, passed)]].set(jnp.asarray(lengths, jnp.int32))

    lengths = jnp.where(number % 4 == 0, named(packed, number // 4), named(common, number - number // 4 - 1))
    mixed = jax.random.permutation(jax.random.fold_in(own, 3), amount)
    giver, taker = mixed[0:amount // 2 * 2:2], mixed[1:amount // 2 * 2:2]
    room = jnp.minimum(lengths[giver] - 1, limit - lengths[taker]) // 2
    room = jnp.where((giver == ranking[0]) | (taker == ranking[0]) | (lengths[taker] == 0), 0, jnp.maximum(room, 0))
    passed = jax.random.randint(jax.random.fold_in(own, 4), (amount // 2,), 0, 1 << 20) % (room + 1)
    lengths = lengths.at[giver].add(-passed).at[taker].add(passed)
    members = jnp.searchsorted(jnp.cumsum(lengths), jnp.arange(rows * top), side="right").astype(jnp.int32)
    listing = members.reshape(top, rows).T
    listing = listing[jax.random.permutation(jax.random.fold_in(own, 1), rows)]
    rotation = jax.random.randint(jax.random.fold_in(own, 2), (rows, 1), 0, top)
    return jnp.take_along_axis(listing, (jnp.arange(top)[None, :] + rotation) % top, axis=1)


def shares(count, total, limit, slope, full):
    portions = [(1 << 20) // math.isqrt(grade ** slope) + 1 for grade in range(1, count + 1)]
    largest = limit if full else min(limit, max(-(-total // count), total * portions[0] // sum(portions)))
    least = 1 if total - largest >= count - 1 else 0
    given, spare = [largest] + [least] * (count - 1), total - largest - least * (count - 1)
    while spare > 0:
        candidates = [i for i in range(1, count) if given[i] < largest] or [i for i in range(1, count) if given[i] < limit]
        mass, budget = sum([portions[i] for i in candidates]), spare
        for i in candidates:
            more = min(limit - given[i], max(1, budget * portions[i] // mass), spare)
            given[i] = given[i] + more
            spare = spare - more
    return np.array(given)


def setup_inputs(seed: int = 0) -> dict:
    streams_of = jax.random.split(jax.random.key(seed), 7)
    query_tokens = draw_query_tokens(jax.random.fold_in(streams_of[6], 71), 0)
    passage_tokens = draw_passage_tokens(jax.random.fold_in(streams_of[6], 71), 0)
    passage_lengths = plant(jax.random.randint(streams_of[2], (PASSAGES,), PLEN // 4, PLEN + 1), jax.random.fold_in(streams_of[2], 1), PLEN // 4, PLEN).astype(jnp.int32)
    cand_shard_keys = jax.random.split(jax.random.fold_in(streams_of[3], 1), QUERIES * CAND // (QRY_GRP * CAND))
    cand_shard_turns = jax.random.permutation(jax.random.fold_in(streams_of[3], 3), QUERIES * CAND // (QRY_GRP * CAND))
    cand_shard = jax.vmap(lambda own, number: deal_out(jax.random.fold_in(streams_of[3], 2), own, number, QRY_GRP * CAND, SHARDS, 1, MOST, 2))(cand_shard_keys, cand_shard_turns).reshape((QUERIES, CAND, 1))
    cand_local = plant(jax.random.randint(streams_of[4], (QUERIES, CAND), 0, PASS_DEV), jax.random.fold_in(streams_of[4], 1), 0, PASS_DEV - 1).astype(jnp.int32)
    teacher_scores = draw_teacher_scores(jax.random.fold_in(streams_of[6], 71), 0)
    return {"query_tokens": query_tokens, "passage_tokens": passage_tokens, "passage_lengths": passage_lengths, "cand_shard": cand_shard, "cand_local": cand_local, "teacher_scores": teacher_scores}


sharpness = 2.0
floor_logit = -1e30


def pair_terms(query_rows, passage_ids, passage_tokens, passage_lengths):
    passage_rows = passage_tokens[passage_ids].astype(jnp.float32)
    sims = jnp.einsum('id,cjd->cij', query_rows.astype(jnp.float32), passage_rows)
    in_length = jnp.arange(PLEN)[None, None, :] < passage_lengths[passage_ids][:, None, None]
    logits = jnp.where(in_length, sharpness * sims, floor_logit)
    row_top = jnp.max(logits, axis=2, keepdims=True)
    exp_terms = jnp.where(in_length, jnp.exp(logits - row_top), 0.0)
    sum_exp = jnp.sum(exp_terms, axis=2, keepdims=True)
    scores = jnp.sum(row_top[..., 0] + jnp.log(sum_exp[..., 0]), axis=1) / sharpness
    weights = (exp_terms / sum_exp).astype(jnp.bfloat16)
    weights = lax.optimization_barrier(weights).astype(jnp.float32)
    return scores, weights, passage_rows


def log_normalize(values):
    row_top = jnp.max(values, axis=1, keepdims=True)
    return values - (row_top + jnp.log(jnp.sum(jnp.exp(values - row_top), axis=1, keepdims=True)))


def reference(query_tokens, passage_tokens, passage_lengths, cand_shard, cand_local, teacher_scores):
    passage_ids = (cand_shard[:, :, 0] * PASS_DEV + cand_local).astype(jnp.int32)

    def score_one(item):
        return pair_terms(item[0], item[1], passage_tokens, passage_lengths)[0]

    student_scores = lax.map(score_one, (query_tokens, passage_ids))
    log_student = log_normalize(student_scores)
    log_teacher = log_normalize(teacher_scores)
    teacher_probs = jnp.exp(log_teacher)
    loss = jnp.sum(teacher_probs * (log_teacher - log_student)) / QUERIES
    coefficient = jnp.exp(log_student) - teacher_probs

    def grad_one(item):
        unused, weights, passage_rows = pair_terms(item[0], item[1], passage_tokens, passage_lengths)
        pair_grads = jnp.einsum('cij,cjd->cid', weights, passage_rows)
        return jnp.sum(item[2][:, None, None] * pair_grads, axis=0)

    query_grads = lax.map(grad_one, (query_tokens, passage_ids, coefficient))
    return (loss, query_grads)
```

```python
import functools
import jax
import jax.numpy as jnp
from jax import lax
from jax.experimental import pallas as pl
from jax.experimental.pallas import tpu as pltpu
from jax.sharding import PartitionSpec as P

LANES = 128
SLOTS = 4
UNROLL = 4
FLOOR = -1e30
NT = (((1,), (1,)), ((), ()))
VMEM = pl.BlockSpec(memory_space=pltpu.VMEM)
SMEM = pl.BlockSpec(memory_space=pltpu.SMEM)
f32 = jnp.float32
bf16 = jnp.bfloat16
i32 = jnp.int32


def call(kernel, outs, in_specs, cost, scratch=()):
    return pl.pallas_call(
        kernel,
        out_shape=outs,
        in_specs=in_specs,
        out_specs=tuple(VMEM for _ in outs),
        scratch_shapes=scratch,
        compiler_params=pltpu.CompilerParams(vmem_limit_bytes=32 * 1024 * 1024),
        cost_estimate=pl.CostEstimate(flops=cost, bytes_accessed=cost // 100, transcendentals=0),
    )


def iota(shape, axis):
    return lax.broadcasted_iota(i32, shape, axis)


def plan(me_ref, shard_ref, local_ref, teacher_ref, lengths_ref, table_ref, slots_ref, count_ref, mass_ref, entropy_ref):
    group, passages = shard_ref.shape[0], lengths_ref.shape[1]
    units = table_ref.shape[1]
    teacher = teacher_ref[...]
    top = jnp.max(teacher, axis=1, keepdims=True)
    log_teacher = teacher - (top + jnp.log(jnp.sum(jnp.exp(teacher - top), axis=1, keepdims=True)))
    probs = jnp.exp(log_teacher)
    entropy_ref[...] = jnp.broadcast_to(jnp.sum(probs * log_teacher, keepdims=True), entropy_ref.shape)
    key = jnp.where(shard_ref[...] == me_ref[0], local_ref[...], -1)
    row = iota((passages, key.shape[1]), 0)
    lane = iota((passages, LANES), 1)
    count = jnp.zeros((passages, LANES), f32)
    mass = jnp.zeros((passages, LANES), f32)
    for q in range(group):
        hit = key[q : q + 1, :] == row
        count = jnp.where(lane == q, jnp.sum(jnp.where(hit, 1.0, 0.0), axis=1, keepdims=True), count)
        mass = jnp.where(lane == q, jnp.sum(jnp.where(hit, probs[q : q + 1, :], 0.0), axis=1, keepdims=True), mass)
    count_ref[...] = count
    mass_ref[...] = mass
    live = count > 0.0
    live_b = jnp.where(live, 1.0, 0.0).astype(bf16)
    before = jnp.where(iota((LANES, LANES), 0) < iota((LANES, LANES), 1), 1.0, 0.0).astype(bf16)
    rank = jnp.dot(live_b, before, preferred_element_type=f32)
    rank = jnp.where(live, rank, -1.0)
    named = lax.dot_general(jnp.ones((8, LANES), bf16), live_b, NT, preferred_element_type=f32)
    needed = ((named.astype(i32) + (SLOTS - 1)) // SLOTS).astype(f32)
    before_p = jnp.where(iota((passages, passages), 0) < iota((passages, passages), 1), 1.0, 0.0).astype(bf16)
    first = jnp.dot(needed.astype(bf16), before_p, preferred_element_type=f32)
    needed, first = needed[0:1, :], first[0:1, :]
    total = jnp.sum(needed, axis=1, keepdims=True)
    unit = iota((units, passages), 0).astype(f32)
    own = (unit >= first) & (unit < first + needed)
    own_f = jnp.where(own, 1.0, 0.0)
    own_b = own_f.astype(bf16)
    passage = jnp.sum(jnp.where(own, iota((units, passages), 1).astype(f32), 0.0), axis=1, keepdims=True)
    length = jnp.sum(jnp.where(own, lengths_ref[...].astype(f32), 0.0), axis=1, keepdims=True)
    offset = jnp.sum(jnp.where(own, unit - first, 0.0), axis=1, keepdims=True) * SLOTS
    wide = iota((units, LANES), 1)
    used = iota((units, LANES), 0).astype(f32) < total
    unit_rank = jnp.where(used, jnp.dot(own_b, rank.astype(bf16), preferred_element_type=f32), -1.0)
    unit_count = jnp.dot(own_b, count.astype(bf16), preferred_element_type=f32)
    unit_mass = jnp.dot(own_f, mass, preferred_element_type=f32, precision=lax.Precision.HIGHEST)
    ints = jnp.where(wide == SLOTS, passage, 0.0)
    ints = jnp.where(wide == SLOTS + 1, length, ints)
    ints = jnp.where(wide == SLOTS + 2, total, ints)
    floats = jnp.zeros((units, LANES), f32)
    wide_f = wide.astype(f32)
    for k in range(SLOTS):
        pick = unit_rank == offset + float(k)
        query = group + jnp.sum(jnp.where(pick, wide_f - group, 0.0), axis=1, keepdims=True)
        ints = jnp.where(wide == k, query, ints)
        floats = jnp.where(wide == k, jnp.sum(jnp.where(pick, unit_count, 0.0), axis=1, keepdims=True), floats)
        floats = jnp.where(wide == SLOTS + k, jnp.sum(jnp.where(pick, unit_mass, 0.0), axis=1, keepdims=True), floats)
    table_ref[...] = jnp.transpose(ints)[: table_ref.shape[0], :].astype(i32)
    slots_ref[...] = jnp.transpose(floats)[: slots_ref.shape[0], :]


def trips(table_ref):
    return (table_ref[SLOTS + 2, 0] + (UNROLL - 1)) // UNROLL


def score(table_ref, query_ref, passage_ref, count_ref, mass_ref, weight_ref, slot_score_ref, local_ref, top_ref, dense_ref):
    group, qlen = query_ref.shape[0], query_ref.shape[1]
    rows, plen = SLOTS * qlen, passage_ref.shape[1]
    dense_ref[...] = jnp.zeros(dense_ref.shape, f32)
    lane = iota((1, LANES), 1)
    column = iota((rows, plen), 1)

    def one(u):
        p, length = table_ref[SLOTS, u], table_ref[SLOTS + 1, u]
        queries = [table_ref[k, u] for k in range(SLOTS)]
        tokens = jnp.concatenate([query_ref[jnp.minimum(q, group - 1)] for q in queries], axis=0)
        logits = lax.dot_general(tokens, passage_ref[p], NT, preferred_element_type=f32)
        logits = jnp.where(column < length, logits, FLOOR)
        top = jnp.max(logits, axis=1, keepdims=True)
        terms = jnp.exp(logits - top)
        total = jnp.sum(terms, axis=1, keepdims=True)
        weight_ref[u] = (terms * (1.0 / total)).astype(bf16)
        tops = jnp.broadcast_to(top, (rows, LANES)).reshape(SLOTS, qlen // 8, 8, LANES)
        totals = jnp.broadcast_to(total, (rows, LANES)).reshape(SLOTS, qlen // 8, 8, LANES)
        sum_top, product = tops[:, 0], totals[:, 0]
        for j in range(1, qlen // 8):
            sum_top, product = sum_top + tops[:, j], product * totals[:, j]
        scores = jnp.sum(sum_top + jnp.log(product), axis=1) * 0.5
        slot_score_ref[u] = scores
        dense = dense_ref[pl.ds(p, 1), :]
        for k in range(SLOTS):
            dense = jnp.where(lane == queries[k], scores[k : k + 1, :], dense)
        dense_ref[pl.ds(p, 1), :] = dense

    def some(t, carry):
        for j in range(UNROLL):
            one(t * UNROLL + j)
        return carry

    lax.fori_loop(0, trips(table_ref), some, 0)
    scores, count, mass = dense_ref[...], count_ref[...], mass_ref[...]
    live = count > 0.0
    top = jnp.max(jnp.where(live, scores, FLOOR), axis=0, keepdims=True)
    gap = jnp.where(live, scores - top, 0.0)
    total = jnp.sum(jnp.where(live, count * jnp.exp(gap), 0.0), axis=0, keepdims=True)
    cross = jnp.sum(mass * gap, axis=0, keepdims=True)
    held = jnp.sum(mass, axis=0, keepdims=True)
    packed = jnp.where(lane < group, top, 0.0)
    for k, part in enumerate((total, cross, held)):
        moved = pltpu.roll(jnp.broadcast_to(part, (8, LANES)), (k + 1) * group, 1)[0:1]
        packed = jnp.where(lane // group == k + 1, moved, packed)
    local_ref[...] = jnp.broadcast_to(packed, local_ref.shape)
    top_ref[...] = jnp.transpose(jnp.broadcast_to(top, (LANES, LANES)))


def terms_of(table_ref, slots_ref, weight_ref, passage_ref, slot_score_ref, top_ref, sums_ref):
    qlen = sums_ref.shape[1] // 2
    sums_ref[...] = jnp.zeros(sums_ref.shape, f32)

    def one(u):
        p = table_ref[SLOTS, u]
        grads = jnp.dot(weight_ref[u], passage_ref[p], preferred_element_type=f32)
        queries = [table_ref[k, u] for k in range(SLOTS)]
        olds = [sums_ref[q] for q in queries]
        for k, q in enumerate(queries):
            part = grads[k * qlen : (k + 1) * qlen]
            student = jnp.exp(slot_score_ref[u, k : k + 1, :] - top_ref[pl.ds(q, 1), :]) * slots_ref[k, u]
            sums_ref[q] = olds[k] + jnp.concatenate([student * part, slots_ref[SLOTS + k, u] * part], axis=0)

    def some(t, carry):
        for j in range(UNROLL):
            one(t * UNROLL + j)
        return carry

    lax.fori_loop(0, trips(table_ref), some, 0)


def join(parts_ref, local_ref, entropy_ref, sums_ref, grads_ref, loss_ref):
    group, qlen = grads_ref.shape[0], grads_ref.shape[1]
    parts = parts_ref[...]
    lane = iota((1, LANES), 1)
    total, cross, held = (pltpu.roll(parts, LANES - (k + 1) * group, 1) for k in range(3))
    top = jnp.max(parts, axis=0, keepdims=True)
    lse = top + jnp.log(jnp.sum(total * jnp.exp(parts - top), axis=0, keepdims=True))
    agreed = jnp.sum(cross + held * (parts - lse), axis=0, keepdims=True)
    agreed = jnp.sum(jnp.where(lane < group, agreed, 0.0), axis=1, keepdims=True)
    loss_ref[...] = jnp.broadcast_to(entropy_ref[...] - agreed, loss_ref.shape)
    factor = jnp.where(lane < group, jnp.exp(local_ref[0:1, :] - lse), 0.0)
    factors = jnp.transpose(jnp.broadcast_to(factor, (LANES, LANES)))
    for q in range(group):
        grads_ref[q] = sums_ref[q, :qlen] * factors[q : q + 1, :] - sums_ref[q, qlen:]


def body(query_tokens, passage_tokens, passage_lengths, cand_shard, cand_local, teacher_scores):
    shards, groups = lax.axis_size("passage"), lax.axis_size("query")
    me = lax.axis_index("passage")
    group, cands = cand_local.shape
    qlen, dim = query_tokens.shape[1:]
    passages, plen, _ = passage_tokens.shape
    units = 176
    padded = 256
    doubled = jnp.broadcast_to(query_tokens * 2, (shards, qlen, dim))
    queries = lax.all_to_all(doubled, "passage", 0, 0, tiled=True)
    lengths = lax.dynamic_slice_in_dim(passage_lengths, me * passages, passages).reshape(1, passages)
    table, slots, count, mass, entropy = call(
        plan,
        (
            jax.ShapeDtypeStruct((16, padded), i32),
            jax.ShapeDtypeStruct((8, padded), f32),
            jax.ShapeDtypeStruct((passages, LANES), f32),
            jax.ShapeDtypeStruct((passages, LANES), f32),
            jax.ShapeDtypeStruct((1, LANES), f32),
        ),
        [SMEM, VMEM, VMEM, VMEM, VMEM],
        int(2e9),
    )(me.reshape(1), cand_shard.reshape(group, cands), cand_local, teacher_scores, lengths)
    weights, slot_scores, local, tops = call(
        score,
        (
            jax.ShapeDtypeStruct((units, SLOTS * qlen, plen), bf16),
            jax.ShapeDtypeStruct((units, SLOTS, LANES), f32),
            jax.ShapeDtypeStruct((8, LANES), f32),
            jax.ShapeDtypeStruct((LANES, LANES), f32),
        ),
        [SMEM, VMEM, VMEM, VMEM, VMEM],
        int(4e9),
        [pltpu.VMEM((passages, LANES), f32)],
    )(table, queries, passage_tokens, count, mass)
    parts = lax.all_to_all(jnp.broadcast_to(local[None, 0:1], (shards, 1, LANES)), "passage", 0, 0, tiled=True)
    (sums,) = call(
        terms_of,
        (jax.ShapeDtypeStruct((group + 1, 2 * qlen, dim), f32),),
        [SMEM, SMEM, VMEM, VMEM, VMEM, VMEM],
        int(4e9),
    )(table, slots, weights, passage_tokens, slot_scores, tops)
    grads, loss = call(
        join,
        (jax.ShapeDtypeStruct((group, qlen, dim), f32), jax.ShapeDtypeStruct((1, LANES), f32)),
        [VMEM, VMEM, VMEM, VMEM],
        int(1e9),
    )(parts.reshape(shards, LANES), local, entropy, sums)
    sent = lax.all_to_all(grads, "passage", 0, 0, tiled=True)
    losses = lax.all_to_all(jnp.broadcast_to(loss[None], (groups, 1, LANES)), "query", 0, 0, tiled=True)
    query_grads = jnp.sum(sent, axis=0, keepdims=True)
    return (jnp.sum(losses[:, 0, 0]) / (groups * group), query_grads)


def solution(mesh):
    placed = (
        P(("query", "passage"), None, None),
        P("passage", None, None),
        P(),
        P("query", None, None),
        P("query", None),
        P("query", None),
    )
    return jax.shard_map(
        body,
        mesh=mesh,
        in_specs=placed,
        out_specs=(P(), P(("query", "passage"), None, None)),
        check_vma=False,
    )
```

```python
import jax
import jax.numpy as jnp
from jax import lax
from jax.experimental import pallas as pl
from jax.experimental.pallas import tpu as pltpu
from jax.sharding import PartitionSpec as P

LANES = 128
SLOTS = 4
UNROLL = 4
FLOOR = -1e30
NT = (((1,), (1,)), ((), ()))
VMEM = pl.BlockSpec(memory_space=pltpu.VMEM)
HBM = pl.BlockSpec(memory_space=pltpu.HBM)
SMEM = pl.BlockSpec(memory_space=pltpu.SMEM)
f32 = jnp.float32
bf16 = jnp.bfloat16
i32 = jnp.int32


def held(shape, dtype):
    return pltpu.VMEM(shape, dtype)


def call(kernel, outs, in_specs, cost, scratch=()):
    return pl.pallas_call(
        kernel,
        out_shape=outs,
        in_specs=in_specs,
        out_specs=tuple(HBM if getattr(o, "memory_space", None) == pltpu.HBM else VMEM for o in outs),
        scratch_shapes=scratch,
        compiler_params=pltpu.CompilerParams(vmem_limit_bytes=24 * 1024 * 1024),
        cost_estimate=pl.CostEstimate(flops=cost, bytes_accessed=cost // 100, transcendentals=0),
    )


def iota(shape, axis):
    return lax.broadcasted_iota(i32, shape, axis)


def plan(me_ref, shard_ref, local_ref, teacher_ref, lengths_ref, table_ref, slot_ref, count_ref, mass_ref, entropy_ref):
    group, passages = shard_ref.shape[0], lengths_ref.shape[1]
    units, padded = count_ref.shape[0], table_ref.shape[1]
    teacher = teacher_ref[...]
    top = jnp.max(teacher, axis=1, keepdims=True)
    log_teacher = teacher - (top + jnp.log(jnp.sum(jnp.exp(teacher - top), axis=1, keepdims=True)))
    probs = jnp.exp(log_teacher)
    entropy_ref[...] = jnp.broadcast_to(jnp.sum(probs * log_teacher, keepdims=True), entropy_ref.shape)
    key = jnp.where(shard_ref[...] == me_ref[0], local_ref[...], -1)
    row = iota((passages, key.shape[1]), 0)
    lane = iota((passages, LANES), 1)
    count = jnp.zeros((passages, LANES), f32)
    mass = jnp.zeros((passages, LANES), f32)
    for q in range(group):
        hit = key[q : q + 1, :] == row
        count = jnp.where(lane == q, jnp.sum(jnp.where(hit, 1.0, 0.0), axis=1, keepdims=True), count)
        mass = jnp.where(lane == q, jnp.sum(jnp.where(hit, probs[q : q + 1, :], 0.0), axis=1, keepdims=True), mass)
    live = count > 0.0
    live_b = jnp.where(live, 1.0, 0.0).astype(bf16)
    before = jnp.where(iota((LANES, LANES), 0) < iota((LANES, LANES), 1), 1.0, 0.0).astype(bf16)
    rank = jnp.dot(live_b, before, preferred_element_type=f32)
    rank = jnp.where(live, rank, -1.0)
    named = lax.dot_general(jnp.ones((8, LANES), bf16), live_b, NT, preferred_element_type=f32)
    needed = ((named.astype(i32) + (SLOTS - 1)) // SLOTS).astype(f32)
    before_p = jnp.where(iota((passages, passages), 0) < iota((passages, passages), 1), 1.0, 0.0).astype(bf16)
    first = jnp.dot(needed.astype(bf16), before_p, preferred_element_type=f32)
    needed, first = needed[0:1, :], first[0:1, :]
    total = jnp.sum(needed, axis=1, keepdims=True)
    unit = iota((padded, passages), 0).astype(f32)
    own = (unit >= first) & (unit < first + needed)
    own_f = jnp.where(own, 1.0, 0.0)
    own_b = own_f.astype(bf16)
    passage = jnp.sum(jnp.where(own, iota((padded, passages), 1).astype(f32), 0.0), axis=1, keepdims=True)
    length = jnp.sum(jnp.where(own, lengths_ref[...].astype(f32), 0.0), axis=1, keepdims=True)
    offset = jnp.sum(jnp.where(own, unit - first, 0.0), axis=1, keepdims=True) * SLOTS
    wide = iota((padded, LANES), 1)
    used = iota((padded, LANES), 0).astype(f32) < total
    unit_rank = jnp.dot(own_b, rank.astype(bf16), preferred_element_type=f32)
    slot = jnp.where(used & (unit_rank >= 0.0), unit_rank - offset, -1.0)
    here = (slot >= 0.0) & (slot < float(SLOTS))
    slot = jnp.where(here, slot, -1.0)
    unit_count = jnp.where(here, jnp.dot(own_b, count.astype(bf16), preferred_element_type=f32), 0.0)
    unit_mass = jnp.dot(own_f, mass, preferred_element_type=f32, precision=lax.Precision.HIGHEST)
    unit_mass = jnp.where(here, unit_mass, 0.0)
    slot_ref[...] = slot[:units]
    count_ref[...] = unit_count[:units]
    mass_ref[...] = unit_mass[:units]
    ints = jnp.where(wide == SLOTS, passage, 0.0)
    ints = jnp.where(wide == SLOTS + 1, length, ints)
    ints = jnp.where(wide == SLOTS + 2, total, ints)
    wide_f = wide.astype(f32)
    for k in range(SLOTS):
        pick = slot == float(k)
        query = group + jnp.sum(jnp.where(pick, wide_f - group, 0.0), axis=1, keepdims=True)
        ints = jnp.where(wide == k, query, ints)
    table_ref[...] = jnp.transpose(ints)[: table_ref.shape[0], :].astype(i32)


def trips(table_ref):
    return (table_ref[SLOTS + 2, 0] + (UNROLL - 1)) // UNROLL


def score(table_ref, query_ref, passage_ref, slot_ref, count_ref, mass_ref, weight_ref, student_ref, local_ref, double_ref, row_ref, buffer_ref, sems):
    group, qlen = query_ref.shape[0], query_ref.shape[1]
    units, plen, columns = weight_ref.shape
    double_ref[...] = query_ref[...] * 2
    row_ref[...] = jnp.zeros(row_ref.shape, f32)
    position = iota((plen, columns), 0)
    rounds = trips(table_ref)

    def out(t):
        return pltpu.make_async_copy(buffer_ref.at[t % 2], weight_ref.at[pl.ds(t * UNROLL, UNROLL)], sems.at[t % 2])

    def some(t, carry):
        @pl.when(t >= 2)
        def _():
            out(t - 2).wait()

        for j in range(UNROLL):
            u = t * UNROLL + j
            p, length = table_ref[SLOTS, u], table_ref[SLOTS + 1, u]
            tokens = jnp.concatenate([double_ref[jnp.minimum(table_ref[k, u], group - 1)] for k in range(SLOTS)], axis=0)
            logits = lax.dot_general(passage_ref[p], tokens, NT, preferred_element_type=f32)
            logits = jnp.where(position < length, logits, FLOOR)
            top = jnp.max(logits, axis=0, keepdims=True)
            terms = jnp.exp(logits - top)
            total = jnp.sum(terms, axis=0, keepdims=True)
            buffer_ref[t % 2, j] = (terms * (1.0 / total)).astype(bf16)
            row_ref[pl.ds(u, 1), :] = top + jnp.log(total)
        out(t).start()
        return carry

    lax.fori_loop(0, rounds, some, 0)
    for back in (2, 1):

        @pl.when(rounds >= back)
        def _():
            out(rounds - back).wait()

    same = iota((columns, LANES), 0) // qlen == iota((columns, LANES), 1)
    summed = jnp.dot(row_ref[...], jnp.where(same, 0.5, 0.0), preferred_element_type=f32, precision=lax.Precision.HIGHEST)
    slot, count, mass = slot_ref[...], count_ref[...], mass_ref[...]
    scores = jnp.zeros((units, LANES), f32)
    for k in range(SLOTS):
        scores = jnp.where(slot == float(k), jnp.broadcast_to(summed[:, k : k + 1], (units, LANES)), scores)
    live = slot >= 0.0
    top = jnp.max(jnp.where(live, scores, FLOOR), axis=0, keepdims=True)
    gap = jnp.where(live, scores - top, 0.0)
    student = jnp.where(live, count * jnp.exp(gap), 0.0)
    student_ref[...] = student
    total = jnp.sum(student, axis=0, keepdims=True)
    cross = jnp.sum(mass * gap, axis=0, keepdims=True)
    kept = jnp.sum(mass, axis=0, keepdims=True)
    lane = iota((1, LANES), 1)
    packed = jnp.where(lane < group, top, 0.0)
    for k, part in enumerate((total, cross, kept)):
        moved = pltpu.roll(jnp.broadcast_to(part, (8, LANES)), (k + 1) * group, 1)[0:1]
        packed = jnp.where(lane // group == k + 1, moved, packed)
    local_ref[...] = jnp.broadcast_to(packed, local_ref.shape)


def terms_of(table_ref, weight_ref, passage_ref, slot_ref, student_ref, mass_ref, sums_ref, factor_ref, buffer_ref, sems):
    qlen = sums_ref.shape[1] // 2
    rounds = trips(table_ref)

    def into(t):
        return pltpu.make_async_copy(weight_ref.at[pl.ds(t * UNROLL, UNROLL)], buffer_ref.at[t % 2], sems.at[t % 2])

    @pl.when(rounds >= 1)
    def _():
        into(0).start()

    sums_ref[...] = jnp.zeros(sums_ref.shape, f32)
    slot = slot_ref[...]
    for k in range(SLOTS):
        for side, values in enumerate((student_ref[...], mass_ref[...])):
            part = jnp.sum(jnp.where(slot == float(k), values, 0.0), axis=1, keepdims=True)
            factor_ref[side * SLOTS + k] = jnp.broadcast_to(part, slot.shape)

    def some(t, carry):
        @pl.when(t + 1 < rounds)
        def _():
            into(t + 1).start()

        into(t).wait()
        for j in range(UNROLL):
            u = t * UNROLL + j
            grads = lax.dot_general(
                buffer_ref[t % 2, j], passage_ref[table_ref[SLOTS, u]], (((0,), (0,)), ((), ())), preferred_element_type=f32
            )
            queries = [table_ref[k, u] for k in range(SLOTS)]
            olds = [sums_ref[q] for q in queries]
            for k, q in enumerate(queries):
                part = grads[k * qlen : (k + 1) * qlen]
                student, share = factor_ref[k, pl.ds(u, 1), :], factor_ref[SLOTS + k, pl.ds(u, 1), :]
                sums_ref[q] = olds[k] + jnp.concatenate([student * part, share * part], axis=0)
        return carry

    lax.fori_loop(0, rounds, some, 0)


def join(parts_ref, local_ref, entropy_ref, sums_ref, grads_ref, loss_ref):
    group, qlen = grads_ref.shape[0], grads_ref.shape[1]
    parts = parts_ref[...]
    lane = iota((1, LANES), 1)
    total, cross, kept = (pltpu.roll(parts, LANES - (k + 1) * group, 1) for k in range(3))
    top = jnp.max(parts, axis=0, keepdims=True)
    lse = top + jnp.log(jnp.sum(total * jnp.exp(parts - top), axis=0, keepdims=True))
    agreed = jnp.sum(cross + kept * (parts - lse), axis=0, keepdims=True)
    agreed = jnp.sum(jnp.where(lane < group, agreed, 0.0), axis=1, keepdims=True)
    loss_ref[...] = jnp.broadcast_to(entropy_ref[...] - agreed, loss_ref.shape)
    factor = jnp.where(lane < group, jnp.exp(local_ref[0:1, :] - lse), 0.0)
    factors = jnp.transpose(jnp.broadcast_to(factor, (LANES, LANES)))
    for q in range(group):
        grads_ref[q] = sums_ref[q, :qlen] * factors[q : q + 1, :] - sums_ref[q, qlen:]


def body(query_tokens, passage_tokens, passage_lengths, cand_shard, cand_local, teacher_scores):
    shards, groups = lax.axis_size("passage"), lax.axis_size("query")
    me = lax.axis_index("passage")
    group, cands = cand_local.shape
    qlen, dim = query_tokens.shape[1:]
    passages, plen, _ = passage_tokens.shape
    units = 176
    padded = 256
    queries = lax.all_to_all(jnp.broadcast_to(query_tokens, (shards, qlen, dim)), "passage", 0, 0, tiled=True)
    lengths = lax.dynamic_slice_in_dim(passage_lengths, me * passages, passages).reshape(1, passages)
    table, slot, count, mass, entropy = call(
        plan,
        (
            held((16, padded), i32),
            held((units, LANES), f32),
            held((units, LANES), f32),
            held((units, LANES), f32),
            held((1, LANES), f32),
        ),
        [SMEM, VMEM, VMEM, VMEM, VMEM],
        int(2e9),
    )(me.reshape(1), cand_shard.reshape(group, cands), cand_local, teacher_scores, lengths)
    weights, student, local = call(
        score,
        (
            pltpu.HBM((units, plen, SLOTS * qlen), bf16),
            held((units, LANES), f32),
            held((8, LANES), f32),
        ),
        [SMEM, VMEM, VMEM, VMEM, VMEM, VMEM],
        int(4e9),
        [
            pltpu.VMEM(queries.shape, bf16),
            pltpu.VMEM((units, LANES), f32),
            pltpu.VMEM((2, UNROLL, plen, SLOTS * qlen), bf16),
            pltpu.SemaphoreType.DMA((2,)),
        ],
    )(table, queries, passage_tokens, slot, count, mass)
    parts = lax.all_to_all(jnp.broadcast_to(local[None, 0:1], (shards, 1, LANES)), "passage", 0, 0, tiled=True)
    (sums,) = call(
        terms_of,
        (held((group + 1, 2 * qlen, dim), f32),),
        [SMEM, HBM, VMEM, VMEM, VMEM, VMEM],
        int(4e9),
        [
            pltpu.VMEM((2 * SLOTS, units, LANES), f32),
            pltpu.VMEM((2, UNROLL, plen, SLOTS * qlen), bf16),
            pltpu.SemaphoreType.DMA((2,)),
        ],
    )(table, weights, passage_tokens, slot, student, mass)
    grads, loss = call(
        join,
        (jax.ShapeDtypeStruct((group, qlen, dim), f32), jax.ShapeDtypeStruct((1, LANES), f32)),
        [VMEM, VMEM, VMEM, VMEM],
        int(1e9),
    )(parts.reshape(shards, LANES), local, entropy, sums)
    sent = lax.all_to_all(grads, "passage", 0, 0, tiled=True)
    side = 4
    near = [[side * a + b for b in range(side)] for a in range(groups // side)]
    far = [[side * a + b for a in range(groups // side)] for b in range(side)]
    loss = lax.psum(lax.psum(loss, "query", axis_index_groups=near), "query", axis_index_groups=far)
    query_grads = jnp.sum(sent, axis=0, keepdims=True)
    return (loss[0, 0] / (groups * group), query_grads)


def solution(mesh):
    placed = (
        P(("query", "passage"), None, None),
        P("passage", None, None),
        P(),
        P("query", None, None),
        P("query", None),
        P("query", None),
    )
    return jax.shard_map(
        body,
        mesh=mesh,
        in_specs=placed,
        out_specs=(P(), P(("query", "passage"), None, None)),
        check_vma=False,
    )
```

```python
import math
import jax
import jax.numpy as jnp
from jax import lax
from jax.experimental import pallas as pl
from jax.experimental.pallas import tpu as pltpu
from jax.sharding import PartitionSpec as P

LANES = 128
SLOTS = 4
UNROLL = 8
UNITS = 176
PLEN = 128
PADDED = 256
PAIR = 2
FLOOR = -1e30
NT = (((1,), (1,)), ((), ()))
VMEM = pl.BlockSpec(memory_space=pltpu.VMEM)
HBM = pl.BlockSpec(memory_space=pltpu.HBM)
SMEM = pl.BlockSpec(memory_space=pltpu.SMEM)
f32 = jnp.float32
bf16 = jnp.bfloat16
i32 = jnp.int32


def held(shape, dtype):
    return pltpu.VMEM(shape, dtype)


def in_hbm(array):
    return pltpu.with_memory_space_constraint(array, pltpu.HBM)


def call(kernel, outs, in_specs, cost, scratch=()):
    return pl.pallas_call(
        kernel,
        out_shape=outs,
        in_specs=in_specs,
        out_specs=tuple(HBM if getattr(o, "memory_space", None) == pltpu.HBM else VMEM for o in outs),
        scratch_shapes=scratch,
        compiler_params=pltpu.CompilerParams(vmem_limit_bytes=24 * 1024 * 1024),
        cost_estimate=pl.CostEstimate(flops=cost, bytes_accessed=cost // 100, transcendentals=0),
    )


def iota(shape, axis):
    return lax.broadcasted_iota(i32, shape, axis)


def plan(me_ref, shard_ref, local_ref, teacher_ref, lengths_ref, table_ref, slot_ref, count_ref, mass_ref, share_ref, entropy_ref):
    group, passages = shard_ref.shape[0], lengths_ref.shape[1]
    units, padded = count_ref.shape[0], PADDED
    teacher = teacher_ref[...]
    top = jnp.max(teacher, axis=1, keepdims=True)
    log_teacher = teacher - (top + jnp.log(jnp.sum(jnp.exp(teacher - top), axis=1, keepdims=True)))
    probs = jnp.exp(log_teacher)
    here = shard_ref[...] == me_ref[0]
    entropy_ref[...] = jnp.broadcast_to(jnp.sum(jnp.where(here, probs * log_teacher, 0.0), keepdims=True), entropy_ref.shape)
    key = jnp.where(here, local_ref[...], -1)
    row = iota((passages, key.shape[1]), 0)
    lane = iota((passages, LANES), 1)
    count = jnp.zeros((passages, LANES), f32)
    mass = jnp.zeros((passages, LANES), f32)
    for q in range(group):
        hit = key[q : q + 1, :] == row
        count = jnp.where(lane == q, jnp.sum(jnp.where(hit, 1.0, 0.0), axis=1, keepdims=True), count)
        mass = jnp.where(lane == q, jnp.sum(jnp.where(hit, probs[q : q + 1, :], 0.0), axis=1, keepdims=True), mass)
    live = count > 0.0
    live_b = jnp.where(live, 1.0, 0.0).astype(bf16)
    before = jnp.where(iota((LANES, LANES), 0) < iota((LANES, LANES), 1), 1.0, 0.0).astype(bf16)
    rank = jnp.dot(live_b, before, preferred_element_type=f32)
    rank = jnp.where(live, rank, -1.0)
    named = lax.dot_general(jnp.ones((8, LANES), bf16), live_b, NT, preferred_element_type=f32)
    needed = ((named.astype(i32) + (SLOTS - 1)) // SLOTS).astype(f32)
    before_p = jnp.where(iota((passages, passages), 0) < iota((passages, passages), 1), 1.0, 0.0).astype(bf16)
    first = jnp.dot(needed.astype(bf16), before_p, preferred_element_type=f32)
    needed, first = needed[0:1, :], first[0:1, :]
    total = jnp.sum(needed, axis=1, keepdims=True)
    unit = iota((padded, passages), 0).astype(f32)
    own = (unit >= first) & (unit < first + needed)
    own_f = jnp.where(own, 1.0, 0.0)
    own_b = own_f.astype(bf16)
    passage = jnp.sum(jnp.where(own, iota((padded, passages), 1).astype(f32), 0.0), axis=1, keepdims=True)
    length = jnp.sum(jnp.where(own, lengths_ref[...].astype(f32), 0.0), axis=1, keepdims=True)
    offset = jnp.sum(jnp.where(own, unit - first, 0.0), axis=1, keepdims=True) * SLOTS
    wide = iota((padded, LANES), 1)
    used = iota((padded, LANES), 0).astype(f32) < total
    unit_rank = jnp.dot(own_b, rank.astype(bf16), preferred_element_type=f32)
    slot = jnp.where(used & (unit_rank >= 0.0), unit_rank - offset, -1.0)
    here = (slot >= 0.0) & (slot < float(SLOTS))
    slot = jnp.where(here, slot, -1.0)
    unit_count = jnp.where(here, jnp.dot(own_b, count.astype(bf16), preferred_element_type=f32), 0.0)
    unit_mass = jnp.dot(own_f, mass, preferred_element_type=f32, precision=lax.Precision.HIGHEST)
    unit_mass = jnp.where(here, unit_mass, 0.0)
    slot_ref[...] = slot[:units]
    count_ref[...] = unit_count[:units]
    mass_ref[...] = unit_mass[:units]
    ints = jnp.where(wide == SLOTS, passage, 0.0)
    eights = jnp.floor(length * 0.125) * 8.0
    ints = jnp.where(wide == SLOTS + 1, PLEN - eights, ints)
    ints = jnp.where(wide == SLOTS + 3, length - eights, ints)
    ints = jnp.where(wide == SLOTS + 2, total, ints)
    wide_f = wide.astype(f32)
    shares = jnp.zeros((units, LANES), f32)
    for k in range(SLOTS):
        pick = slot == float(k)
        query = group + jnp.sum(jnp.where(pick, wide_f - group, 0.0), axis=1, keepdims=True)
        ints = jnp.where(wide == k, query, ints)
        share = jnp.sum(jnp.where(pick, unit_mass, 0.0)[:units], axis=1, keepdims=True)
        shares = jnp.where(wide[:units] == SLOTS + k, share, shares)
    share_ref[...] = shares
    ints = jnp.transpose(ints).astype(i32)
    for k in range(SLOTS + 4):
        for half in range(padded // LANES):
            table_ref[pl.ds(k * (padded // LANES) + half, 1), :] = ints[k : k + 1, half * LANES : (half + 1) * LANES]


def field(k):
    return k * PADDED


def trips(table_ref):
    return (table_ref[field(SLOTS + 2)] + (UNROLL - 1)) // UNROLL


def score(
    table_ref, query_ref, passage_ref, slot_ref, count_ref, mass_ref, share_ref, entropy_ref,
    weight_ref, factor_ref, local_ref,
    double_ref, row_ref, logits_ref, buffer_ref, scale_ref, cap_ref, sems,
):
    group, qlen = query_ref.shape[0], query_ref.shape[1]
    units, columns, plen = weight_ref.shape
    double_ref[:group] = query_ref[...] * 2
    double_ref[group] = jnp.zeros(double_ref.shape[1:], bf16)
    row_ref[...] = jnp.zeros(row_ref.shape, f32)
    logits_ref[...] = jnp.zeros(logits_ref.shape, f32)
    for part in range(8):
        cap_ref[part] = jnp.where(iota((2 * plen, columns), 0) < plen + part, -FLOOR, FLOOR)
    rounds = trips(table_ref)

    def out(t):
        first = pl.multiple_of(t * UNROLL, UNROLL)
        return pltpu.make_async_copy(
            buffer_ref.at[pl.ds(first + UNROLL, UNROLL)], weight_ref.at[pl.ds(first, UNROLL)], sems.at[t]
        )

    def some(t, carry):
        for j in range(UNROLL):
            u = t * UNROLL + j
            old = logits_ref[j]
            p = table_ref[field(SLOTS) + u]
            tokens = jnp.concatenate([double_ref[table_ref[field(k) + u]] for k in range(SLOTS)], axis=0)
            logits = lax.dot_general(passage_ref[p], tokens, NT, preferred_element_type=f32)
            start = pl.multiple_of(table_ref[field(SLOTS + 1) + u], 8)
            logits_ref[j] = jnp.minimum(logits, cap_ref[table_ref[field(SLOTS + 3) + u], pl.ds(start, plen), :])
            top = jnp.max(old, axis=0, keepdims=True)
            terms = jnp.exp(old - top)
            total = jnp.sum(terms, axis=0, keepdims=True)
            buffer_ref[u] = jnp.transpose((terms * (1.0 / total)).astype(bf16))
            row_ref[pl.ds(u, 1), :] = top + jnp.log(total)

        @pl.when(t > 0)
        def _():
            out(t - 1).start()

        return carry

    lax.fori_loop(0, rounds + 1, some, 0)
    same = iota((columns, LANES), 0) // qlen == iota((columns, LANES), 1)
    rows = row_ref[pl.ds(UNROLL, units), :]
    summed = jnp.dot(rows, jnp.where(same, 0.5, 0.0), preferred_element_type=f32, precision=lax.Precision.HIGHEST)
    slot, count, mass = slot_ref[...], count_ref[...], mass_ref[...]
    scores = jnp.zeros((units, LANES), f32)
    for k in range(SLOTS):
        scores = jnp.where(slot == float(k), jnp.broadcast_to(summed[:, k : k + 1], (units, LANES)), scores)
    live = slot >= 0.0
    top = jnp.max(jnp.where(live, scores, FLOOR), axis=0, keepdims=True)
    gap = jnp.where(live, scores - top, 0.0)
    student = jnp.where(live, count * jnp.exp(gap), 0.0)
    scale = share_ref[...]
    wide = iota((units, LANES), 1)
    for k in range(SLOTS):
        scale = jnp.where(wide == k, jnp.sum(jnp.where(slot == float(k), student, 0.0), axis=1, keepdims=True), scale)
    scale_ref[...] = scale
    factors = pltpu.make_async_copy(scale_ref, factor_ref, sems.at[units // UNROLL])
    factors.start()
    total = jnp.sum(student, axis=0, keepdims=True)
    lane = iota((1, LANES), 1)
    cross = jnp.sum(mass * gap, axis=0, keepdims=True) - jnp.where(lane == 0, entropy_ref[...], 0.0)
    kept = jnp.sum(mass, axis=0, keepdims=True)
    packed = jnp.where(lane < group, top, 0.0)
    for k, part in enumerate((total, cross, kept)):
        moved = pltpu.roll(jnp.broadcast_to(part, (8, LANES)), (k + 1) * group, 1)[0:1]
        packed = jnp.where(lane // group == k + 1, moved, packed)
    local_ref[...] = jnp.broadcast_to(packed, local_ref.shape)

    def finish(t, carry):
        out(t).wait()
        return carry

    lax.fori_loop(0, rounds, finish, 0)
    factors.wait()


def terms_of(table_ref, weight_ref, passage_ref, factor_ref, sums_ref, scale_ref, spread_ref, grads_ref, buffer_ref, sems):
    qlen = sums_ref.shape[1] // 2
    units = weight_ref.shape[0]
    rounds = trips(table_ref)
    factors = pltpu.make_async_copy(factor_ref, scale_ref, sems.at[units // UNROLL])
    factors.start()

    def into(t):
        part = pl.ds(pl.multiple_of(t * UNROLL, UNROLL), UNROLL)
        return pltpu.make_async_copy(weight_ref.at[part], buffer_ref.at[part], sems.at[t])

    def begin(t, carry):
        into(t).start()
        return carry

    lax.fori_loop(0, rounds, begin, 0)
    sums_ref[...] = jnp.zeros(sums_ref.shape, f32)
    grads_ref[...] = jnp.zeros(grads_ref.shape, f32)
    factors.wait()
    scale = scale_ref[...]
    for k in range(2 * SLOTS):
        spread_ref[k] = jnp.broadcast_to(scale[:, k : k + 1], scale.shape)

    def some(t, carry):
        @pl.when(t < rounds)
        def _():
            into(t).wait()

        for j in range(UNROLL):
            old = grads_ref[j]
            late = jnp.minimum(t, rounds - 1) * UNROLL + j
            grads_ref[j] = jnp.dot(buffer_ref[late], passage_ref[table_ref[field(SLOTS) + late]], preferred_element_type=f32)
            u = jnp.maximum(t - 1, 0) * UNROLL + j
            queries = [table_ref[field(k) + u] for k in range(SLOTS)]
            sums = [sums_ref[q] for q in queries]
            for k, q in enumerate(queries):
                part = old[k * qlen : (k + 1) * qlen]
                student, share = spread_ref[k, pl.ds(u, 1), :], spread_ref[SLOTS + k, pl.ds(u, 1), :]
                sums_ref[q] = sums[k] + jnp.concatenate([student * part, share * part], axis=0)
        return carry

    @pl.when(rounds > 0)
    def _():
        lax.fori_loop(0, rounds + 1, some, 0)


def join(side_ref, parts_ref, local_ref, sums_ref, grads_ref, loss_ref):
    group, qlen = grads_ref.shape[0], grads_ref.shape[1]
    lane = iota((1, LANES), 1)
    loss = jnp.zeros((1, 1), f32)
    lses = []
    for side in range(parts_ref.shape[0] // group):
        parts = parts_ref[side * group : (side + 1) * group]
        total, cross, kept = (pltpu.roll(parts, LANES - (k + 1) * group, 1) for k in range(3))
        top = jnp.max(parts, axis=0, keepdims=True)
        lse = top + jnp.log(jnp.sum(total * jnp.exp(parts - top), axis=0, keepdims=True))
        agreed = jnp.sum(cross + kept * (parts - lse), axis=0, keepdims=True)
        loss = loss - jnp.sum(jnp.where(lane < group, agreed, 0.0), axis=1, keepdims=True)
        lses.append(lse)
    loss_ref[...] = jnp.broadcast_to(loss, loss_ref.shape)
    lse = lses[0]
    for side in range(1, len(lses)):
        lse = jnp.where(side_ref[0] == side, lses[side], lse)
    factor = jnp.where(lane < group, jnp.exp(local_ref[0:1, :] - lse), 0.0)
    factors = jnp.transpose(jnp.broadcast_to(factor, (LANES, LANES)))
    for q in range(group):
        grads_ref[q] = sums_ref[q, :qlen] * factors[q : q + 1, :] - sums_ref[q, qlen:]


def body(query_tokens, passage_tokens, passage_lengths, cand_shard, cand_local, teacher_scores):
    shards, groups = lax.axis_size("passage"), lax.axis_size("query")
    me, own = lax.axis_index("passage"), lax.axis_index("query")
    group, cands = cand_local.shape
    qlen, dim = query_tokens.shape[1:]
    passages, plen, _ = passage_tokens.shape
    units = UNITS
    queries = lax.all_to_all(jnp.broadcast_to(query_tokens, (shards, qlen, dim)), "passage", 0, 0, tiled=True)
    lengths = lax.dynamic_slice_in_dim(passage_lengths, me * passages, passages).reshape(1, passages)
    table, slot, count, mass, share, entropy = call(
        plan,
        (
            held((2 * SLOTS * PADDED // LANES, LANES), i32),
            held((units, LANES), f32),
            held((units, LANES), f32),
            held((units, LANES), f32),
            held((units, LANES), f32),
            held((1, LANES), f32),
        ),
        [SMEM, VMEM, VMEM, VMEM, VMEM],
        int(2e9),
    )(me.reshape(1), cand_shard.reshape(group, cands), cand_local, teacher_scores, lengths)
    weights, factors, local = call(
        score,
        (
            pltpu.HBM((units, SLOTS * qlen, plen), bf16),
            pltpu.HBM((units, LANES), f32),
            held((PAIR * shards, LANES), f32),
        ),
        [SMEM, VMEM, VMEM, VMEM, VMEM, VMEM, VMEM, VMEM],
        int(4e9),
        [
            pltpu.VMEM((group + 1, qlen, dim), bf16),
            pltpu.VMEM((UNROLL + units, LANES), f32),
            pltpu.VMEM((UNROLL, plen, SLOTS * qlen), f32),
            pltpu.VMEM((UNROLL + units, SLOTS * qlen, plen), bf16),
            pltpu.VMEM((units, LANES), f32),
            pltpu.VMEM((8, 2 * plen, SLOTS * qlen), f32),
            pltpu.SemaphoreType.DMA((units // UNROLL + 1,)),
        ],
    )(table.reshape(-1), queries, passage_tokens, slot, count, mass, share, entropy)
    pairs = [[g * shards + s for g in range(a, a + PAIR) for s in range(shards)] for a in range(0, groups, PAIR)]
    parts = lax.all_to_all(
        local.reshape(PAIR * shards, 1, LANES), ("query", "passage"), 0, 0, tiled=True, axis_index_groups=pairs
    )
    (sums,) = call(
        terms_of,
        (held((group + 1, 2 * qlen, dim), f32),),
        [SMEM, HBM, VMEM, HBM],
        int(4e9),
        [
            pltpu.VMEM((units, LANES), f32),
            pltpu.VMEM((2 * SLOTS, units, LANES), f32),
            pltpu.VMEM((UNROLL, SLOTS * qlen, dim), f32),
            pltpu.VMEM((units, SLOTS * qlen, plen), bf16),
            pltpu.SemaphoreType.DMA((units // UNROLL + 1,)),
        ],
    )(table.reshape(-1), in_hbm(weights), passage_tokens, in_hbm(factors))
    grads, loss = call(
        join,
        (jax.ShapeDtypeStruct((group, qlen, dim), f32), jax.ShapeDtypeStruct((1, LANES), f32)),
        [SMEM, VMEM, VMEM, VMEM],
        int(1e9),
    )((own % PAIR).reshape(1), parts.reshape(PAIR * shards, LANES), local, sums)
    sent = lax.all_to_all(grads, "passage", 0, 0, tiled=True)
    rings = [list(range(a, groups, PAIR)) for a in range(PAIR)]
    loss = lax.psum(loss, "query", axis_index_groups=rings)
    query_grads = jnp.sum(sent, axis=0, keepdims=True)
    return (loss[0, 0] / (groups * group), query_grads)


def solution(mesh):
    placed = (
        P(("query", "passage"), None, None),
        P("passage", None, None),
        P(),
        P("query", None, None),
        P("query", None),
        P("query", None),
    )
    return jax.shard_map(
        body,
        mesh=mesh,
        in_specs=placed,
        out_specs=(P(), P(("query", "passage"), None, None)),
        check_vma=False,
    )
```

```python
import math
import jax
import jax.numpy as jnp
from jax import lax
from jax.experimental import pallas as pl
from jax.experimental.pallas import tpu as pltpu
from jax.sharding import PartitionSpec as P

LANES = 128
SLOTS = 4
UNROLL = 8
UNITS = 176
PLEN = 128
PADDED = 256
TOLD = 4
FLOOR = -1e30
NT = (((1,), (1,)), ((), ()))
VMEM = pl.BlockSpec(memory_space=pltpu.VMEM)
HBM = pl.BlockSpec(memory_space=pltpu.HBM)
SMEM = pl.BlockSpec(memory_space=pltpu.SMEM)
f32 = jnp.float32
bf16 = jnp.bfloat16
i32 = jnp.int32


def held(shape, dtype):
    return pltpu.VMEM(shape, dtype)


def in_hbm(array):
    return pltpu.with_memory_space_constraint(array, pltpu.HBM)


def call(kernel, outs, in_specs, cost, scratch=()):
    return pl.pallas_call(
        kernel,
        out_shape=outs,
        in_specs=in_specs,
        out_specs=tuple(HBM if getattr(o, "memory_space", None) == pltpu.HBM else VMEM for o in outs),
        scratch_shapes=scratch,
        compiler_params=pltpu.CompilerParams(vmem_limit_bytes=24 * 1024 * 1024),
        cost_estimate=pl.CostEstimate(flops=cost, bytes_accessed=cost // 100, transcendentals=0),
    )


def iota(shape, axis):
    return lax.broadcasted_iota(i32, shape, axis)


def plan(shard_ref, local_ref, teacher_ref, lengths_ref, table_ref, slot_ref, count_ref, mass_ref, share_ref, entropy_ref):
    group, passages = shard_ref.shape[0], lengths_ref.shape[1]
    units, padded = count_ref.shape[0], PADDED
    teacher = teacher_ref[...]
    top = jnp.max(teacher, axis=1, keepdims=True)
    log_teacher = teacher - (top + jnp.log(jnp.sum(jnp.exp(teacher - top), axis=1, keepdims=True)))
    probs = jnp.exp(log_teacher)
    here = shard_ref[...] == lax.axis_index("passage")
    entropy_ref[...] = jnp.broadcast_to(jnp.sum(jnp.where(here, probs * log_teacher, 0.0), keepdims=True), entropy_ref.shape)
    key = jnp.where(here, local_ref[...], -1)
    row = iota((passages, key.shape[1]), 0)
    lane = iota((passages, LANES), 1)
    count = jnp.zeros((passages, LANES), f32)
    mass = jnp.zeros((passages, LANES), f32)
    for q in range(group):
        hit = key[q : q + 1, :] == row
        count = jnp.where(lane == q, jnp.sum(jnp.where(hit, 1.0, 0.0), axis=1, keepdims=True), count)
        mass = jnp.where(lane == q, jnp.sum(jnp.where(hit, probs[q : q + 1, :], 0.0), axis=1, keepdims=True), mass)
    live = count > 0.0
    live_b = jnp.where(live, 1.0, 0.0).astype(bf16)
    before = jnp.where(iota((LANES, LANES), 0) < iota((LANES, LANES), 1), 1.0, 0.0).astype(bf16)
    rank = jnp.dot(live_b, before, preferred_element_type=f32)
    rank = jnp.where(live, rank, -1.0)
    named = lax.dot_general(jnp.ones((8, LANES), bf16), live_b, NT, preferred_element_type=f32)
    needed = ((named.astype(i32) + (SLOTS - 1)) // SLOTS).astype(f32)
    before_p = jnp.where(iota((passages, passages), 0) < iota((passages, passages), 1), 1.0, 0.0).astype(bf16)
    first = jnp.dot(needed.astype(bf16), before_p, preferred_element_type=f32)
    needed, first = needed[0:1, :], first[0:1, :]
    total = jnp.sum(needed, axis=1, keepdims=True)
    unit = iota((padded, passages), 0).astype(f32)
    own = (unit >= first) & (unit < first + needed)
    own_f = jnp.where(own, 1.0, 0.0)
    own_b = own_f.astype(bf16)
    passage = jnp.sum(jnp.where(own, iota((padded, passages), 1).astype(f32), 0.0), axis=1, keepdims=True)
    length = jnp.sum(jnp.where(own, lengths_ref[...].astype(f32), 0.0), axis=1, keepdims=True)
    offset = jnp.sum(jnp.where(own, unit - first, 0.0), axis=1, keepdims=True) * SLOTS
    wide = iota((padded, LANES), 1)
    used = iota((padded, LANES), 0).astype(f32) < total
    unit_rank = jnp.dot(own_b, rank.astype(bf16), preferred_element_type=f32)
    slot = jnp.where(used & (unit_rank >= 0.0), unit_rank - offset, -1.0)
    here = (slot >= 0.0) & (slot < float(SLOTS))
    slot = jnp.where(here, slot, -1.0)
    unit_count = jnp.where(here, jnp.dot(own_b, count.astype(bf16), preferred_element_type=f32), 0.0)
    unit_mass = jnp.dot(own_f, mass, preferred_element_type=f32, precision=lax.Precision.HIGHEST)
    unit_mass = jnp.where(here, unit_mass, 0.0)
    slot_ref[...] = slot[:units]
    count_ref[...] = unit_count[:units]
    mass_ref[...] = unit_mass[:units]
    ints = jnp.where(wide == SLOTS, passage, 0.0)
    eights = jnp.floor(length * 0.125) * 8.0
    ints = jnp.where(wide == SLOTS + 1, PLEN - eights, ints)
    ints = jnp.where(wide == SLOTS + 3, length - eights, ints)
    ints = jnp.where(wide == SLOTS + 2, total, ints)
    wide_f = wide.astype(f32)
    shares = jnp.zeros((units, LANES), f32)
    for k in range(SLOTS):
        pick = slot == float(k)
        query = group + jnp.sum(jnp.where(pick, wide_f - group, 0.0), axis=1, keepdims=True)
        ints = jnp.where(wide == k, query, ints)
        share = jnp.sum(jnp.where(pick, unit_mass, 0.0)[:units], axis=1, keepdims=True)
        shares = jnp.where(wide[:units] == SLOTS + k, share, shares)
    share_ref[...] = shares
    ints = jnp.transpose(ints).astype(i32)
    for k in range(SLOTS + 4):
        for half in range(padded // LANES):
            table_ref[pl.ds(k * (padded // LANES) + half, 1), :] = ints[k : k + 1, half * LANES : (half + 1) * LANES]


def field(k):
    return k * PADDED


def trips(table_ref):
    return (table_ref[field(SLOTS + 2)] + (UNROLL - 1)) // UNROLL


def score(
    table_ref, query_ref, passage_ref, slot_ref, count_ref, mass_ref, share_ref, entropy_ref,
    weight_ref, factor_ref, local_ref,
    double_ref, row_ref, logits_ref, buffer_ref, scale_ref, cap_ref, sems,
):
    group, qlen = query_ref.shape[0], query_ref.shape[1]
    units, columns, plen = weight_ref.shape
    double_ref[:group] = query_ref[...] * 2
    double_ref[group] = jnp.zeros(double_ref.shape[1:], bf16)
    row_ref[...] = jnp.zeros(row_ref.shape, f32)
    logits_ref[...] = jnp.zeros(logits_ref.shape, f32)
    for part in range(8):
        cap_ref[part] = jnp.where(iota((2 * plen, columns), 0) < plen + part, -FLOOR, FLOOR)
    rounds = trips(table_ref)

    def out(t):
        first = pl.multiple_of(t * UNROLL, UNROLL)
        return pltpu.make_async_copy(
            buffer_ref.at[pl.ds(first + UNROLL, UNROLL)], weight_ref.at[pl.ds(first, UNROLL)], sems.at[t]
        )

    def some(t, carry):
        for j in range(UNROLL):
            u = t * UNROLL + j
            old = logits_ref[j]
            p = table_ref[field(SLOTS) + u]
            tokens = jnp.concatenate([double_ref[table_ref[field(k) + u]] for k in range(SLOTS)], axis=0)
            logits = lax.dot_general(passage_ref[p], tokens, NT, preferred_element_type=f32)
            start = pl.multiple_of(table_ref[field(SLOTS + 1) + u], 8)
            logits_ref[j] = jnp.minimum(logits, cap_ref[table_ref[field(SLOTS + 3) + u], pl.ds(start, plen), :])
            top = jnp.max(old, axis=0, keepdims=True)
            terms = jnp.exp(old - top)
            total = jnp.sum(terms, axis=0, keepdims=True)
            buffer_ref[u] = jnp.transpose((terms * (1.0 / total)).astype(bf16))
            row_ref[pl.ds(u, 1), :] = top + jnp.log(total)

        @pl.when(t > 0)
        def _():
            out(t - 1).start()

        return carry

    lax.fori_loop(0, rounds + 1, some, 0)
    same = iota((columns, LANES), 0) // qlen == iota((columns, LANES), 1)
    rows = row_ref[pl.ds(UNROLL, units), :]
    summed = jnp.dot(rows, jnp.where(same, 0.5, 0.0), preferred_element_type=f32, precision=lax.Precision.HIGHEST)
    slot, count, mass = slot_ref[...], count_ref[...], mass_ref[...]
    scores = jnp.zeros((units, LANES), f32)
    for k in range(SLOTS):
        scores = jnp.where(slot == float(k), jnp.broadcast_to(summed[:, k : k + 1], (units, LANES)), scores)
    live = slot >= 0.0
    top = jnp.max(jnp.where(live, scores, FLOOR), axis=0, keepdims=True)
    gap = jnp.where(live, scores - top, 0.0)
    student = jnp.where(live, count * jnp.exp(gap), 0.0)
    scale = share_ref[...]
    wide = iota((units, LANES), 1)
    for k in range(SLOTS):
        scale = jnp.where(wide == k, jnp.sum(jnp.where(slot == float(k), student, 0.0), axis=1, keepdims=True), scale)
    scale_ref[...] = scale
    factors = pltpu.make_async_copy(scale_ref, factor_ref, sems.at[units // UNROLL])
    factors.start()
    total = jnp.sum(student, axis=0, keepdims=True)
    lane = iota((1, LANES), 1)
    cross = jnp.sum(mass * gap, axis=0, keepdims=True) - jnp.where(lane == 0, entropy_ref[...], 0.0)
    kept = jnp.sum(mass, axis=0, keepdims=True)
    packed = jnp.where(lane < group, top, 0.0)
    for k, part in enumerate((total, cross, kept)):
        moved = pltpu.roll(jnp.broadcast_to(part, (8, LANES)), (k + 1) * group, 1)[0:1]
        packed = jnp.where(lane // group == k + 1, moved, packed)
    local_ref[...] = jnp.broadcast_to(packed, local_ref.shape)

    def finish(t, carry):
        out(t).wait()
        return carry

    lax.fori_loop(0, rounds, finish, 0)
    factors.wait()


def terms_of(table_ref, weight_ref, passage_ref, factor_ref, sums_ref, scale_ref, spread_ref, grads_ref, buffer_ref, sems):
    qlen = sums_ref.shape[1] // 2
    units = weight_ref.shape[0]
    rounds = trips(table_ref)
    factors = pltpu.make_async_copy(factor_ref, scale_ref, sems.at[units // UNROLL])
    factors.start()

    def into(t):
        part = pl.ds(pl.multiple_of(t * UNROLL, UNROLL), UNROLL)
        return pltpu.make_async_copy(weight_ref.at[part], buffer_ref.at[part], sems.at[t])

    def begin(t, carry):
        into(t).start()
        return carry

    lax.fori_loop(0, rounds, begin, 0)
    sums_ref[...] = jnp.zeros(sums_ref.shape, f32)
    grads_ref[...] = jnp.zeros(grads_ref.shape, f32)
    factors.wait()
    scale = scale_ref[...]
    for k in range(2 * SLOTS):
        spread_ref[k] = jnp.broadcast_to(scale[:, k : k + 1], scale.shape)

    def some(t, carry):
        @pl.when(t < rounds)
        def _():
            into(t).wait()

        for j in range(UNROLL):
            old = grads_ref[j]
            late = jnp.minimum(t, rounds - 1) * UNROLL + j
            grads_ref[j] = jnp.dot(buffer_ref[late], passage_ref[table_ref[field(SLOTS) + late]], preferred_element_type=f32)
            u = jnp.maximum(t - 1, 0) * UNROLL + j
            queries = [table_ref[field(k) + u] for k in range(SLOTS)]
            sums = [sums_ref[q] for q in queries]
            for k, q in enumerate(queries):
                part = old[k * qlen : (k + 1) * qlen]
                student, share = spread_ref[k, pl.ds(u, 1), :], spread_ref[SLOTS + k, pl.ds(u, 1), :]
                sums_ref[q] = sums[k] + jnp.concatenate([student * part, share * part], axis=0)
        return carry

    @pl.when(rounds > 0)
    def _():
        lax.fori_loop(0, rounds + 1, some, 0)


def shared(parts):
    group = LANES // 4
    total, cross, kept = (pltpu.roll(parts, LANES - (k + 1) * group, 1) for k in range(3))
    top = jnp.max(parts, axis=0, keepdims=True)
    lse = top + jnp.log(jnp.sum(total * jnp.exp(parts - top), axis=0, keepdims=True))
    return lse, cross, kept


def losses(parts_ref, loss_ref):
    shards = parts_ref.shape[0] // TOLD
    loss = jnp.zeros((1, 1), f32)
    for side in range(TOLD):
        parts = parts_ref[side * shards : (side + 1) * shards]
        lse, cross, kept = shared(parts)
        agreed = jnp.sum(cross + kept * (parts - lse), axis=0, keepdims=True)
        loss = loss - jnp.sum(jnp.where(iota((1, LANES), 1) < LANES // 4, agreed, 0.0), axis=1, keepdims=True)
    loss_ref[...] = jnp.broadcast_to(loss, loss_ref.shape)


def join(parts_ref, local_ref, sums_ref, grads_ref):
    group, qlen = grads_ref.shape[0], grads_ref.shape[1]
    shards = parts_ref.shape[0] // TOLD
    own = lax.axis_index("query")
    side = own // (lax.axis_size("query") // 2) * 2 + own % 2
    lse = shared(parts_ref[pl.ds(pl.multiple_of(side * shards, 8), shards), :])[0]
    factor = jnp.where(iota((1, LANES), 1) < group, jnp.exp(local_ref[0:1, :] - lse), 0.0)
    factors = jnp.transpose(jnp.broadcast_to(factor, (LANES, LANES)))
    for q in range(group):
        grads_ref[q] = sums_ref[q, :qlen] * factors[q : q + 1, :] - sums_ref[q, qlen:]


def body(query_tokens, passage_tokens, passage_lengths, cand_shard, cand_local, teacher_scores):
    shards, groups = lax.axis_size("passage"), lax.axis_size("query")
    me = lax.axis_index("passage")
    group, cands = cand_local.shape
    qlen, dim = query_tokens.shape[1:]
    passages, plen, _ = passage_tokens.shape
    units = UNITS
    queries = lax.all_to_all(jnp.broadcast_to(query_tokens, (shards, qlen, dim)), "passage", 0, 0, tiled=True)
    lengths = lax.dynamic_slice_in_dim(passage_lengths, me * passages, passages).reshape(1, passages)
    table, slot, count, mass, share, entropy = call(
        plan,
        (
            held((2 * SLOTS * PADDED // LANES, LANES), i32),
            held((units, LANES), f32),
            held((units, LANES), f32),
            held((units, LANES), f32),
            held((units, LANES), f32),
            held((1, LANES), f32),
        ),
        [VMEM, VMEM, VMEM, VMEM],
        int(2e9),
    )(cand_shard.reshape(group, cands), cand_local, teacher_scores, lengths)
    weights, factors, local = call(
        score,
        (
            pltpu.HBM((units, SLOTS * qlen, plen), bf16),
            pltpu.HBM((units, LANES), f32),
            held((TOLD * shards, LANES), f32),
        ),
        [SMEM, VMEM, VMEM, VMEM, VMEM, VMEM, VMEM, VMEM],
        int(4e9),
        [
            pltpu.VMEM((group + 1, qlen, dim), bf16),
            pltpu.VMEM((UNROLL + units, LANES), f32),
            pltpu.VMEM((UNROLL, plen, SLOTS * qlen), f32),
            pltpu.VMEM((UNROLL + units, SLOTS * qlen, plen), bf16),
            pltpu.VMEM((units, LANES), f32),
            pltpu.VMEM((8, 2 * plen, SLOTS * qlen), f32),
            pltpu.SemaphoreType.DMA((units // UNROLL + 1,)),
        ],
    )(table.reshape(-1), queries, passage_tokens, slot, count, mass, share, entropy)
    told = [[a + c + h * groups // 2 for h in range(2) for c in range(2)] for a in range(0, groups // 2, 2)]
    sets = [[g * shards + s for g in members for s in range(shards)] for members in told]
    parts = lax.all_to_all(
        local.reshape(TOLD * shards, 1, LANES), ("query", "passage"), 0, 0, tiled=True, axis_index_groups=sets
    )
    (sums,) = call(
        terms_of,
        (held((group + 1, 2 * qlen, dim), f32),),
        [SMEM, HBM, VMEM, HBM],
        int(4e9),
        [
            pltpu.VMEM((units, LANES), f32),
            pltpu.VMEM((2 * SLOTS, units, LANES), f32),
            pltpu.VMEM((UNROLL, SLOTS * qlen, dim), f32),
            pltpu.VMEM((units, SLOTS * qlen, plen), bf16),
            pltpu.SemaphoreType.DMA((units // UNROLL + 1,)),
        ],
    )(table.reshape(-1), in_hbm(weights), passage_tokens, in_hbm(factors))
    parts = parts.reshape(TOLD * shards, LANES)
    (grads,) = call(
        join, (jax.ShapeDtypeStruct((group, qlen, dim), f32),), [VMEM, VMEM, VMEM], int(1e9)
    )(parts, local, sums)
    (loss,) = call(losses, (jax.ShapeDtypeStruct((1, LANES), f32),), [VMEM], int(1e9))(parts)
    sent = lax.all_to_all(grads, "passage", 0, 0, tiled=True)
    left = [list(members) for members in zip(*told)]
    loss = lax.psum(loss, "query", axis_index_groups=left)
    query_grads = jnp.sum(sent, axis=0, keepdims=True)
    return (loss[0, 0] / (groups * group), query_grads)


def solution(mesh):
    placed = (
        P(("query", "passage"), None, None),
        P("passage", None, None),
        P(),
        P("query", None, None),
        P("query", None),
        P("query", None),
    )
    return jax.shard_map(
        body,
        mesh=mesh,
        in_specs=placed,
        out_specs=(P(), P(("query", "passage"), None, None)),
        check_vma=False,
    )
```

```python
import math
import jax
import jax.numpy as jnp
from jax import lax
from jax.experimental import pallas as pl
from jax.experimental.pallas import tpu as pltpu
from jax.sharding import PartitionSpec as P

LANES = 128
SLOTS = 4
AHEAD = 16
UNROLL = 8
UNITS = 176
PLEN = 128
PADDED = 256
TOLD = 2
FLOOR = -1e30
NT = (((1,), (1,)), ((), ()))
VMEM = pl.BlockSpec(memory_space=pltpu.VMEM)
HBM = pl.BlockSpec(memory_space=pltpu.HBM)
SMEM = pl.BlockSpec(memory_space=pltpu.SMEM)
f32 = jnp.float32
bf16 = jnp.bfloat16
i32 = jnp.int32


def held(shape, dtype):
    return pltpu.VMEM(shape, dtype)


def in_hbm(array):
    return pltpu.with_memory_space_constraint(array, pltpu.HBM)


def call(kernel, outs, in_specs, cost, scratch=()):
    return pl.pallas_call(
        kernel,
        out_shape=outs,
        in_specs=in_specs,
        out_specs=tuple(HBM if getattr(o, "memory_space", None) == pltpu.HBM else VMEM for o in outs),
        scratch_shapes=scratch,
        compiler_params=pltpu.CompilerParams(vmem_limit_bytes=24 * 1024 * 1024),
        cost_estimate=pl.CostEstimate(flops=cost, bytes_accessed=cost // 100, transcendentals=0),
    )


def iota(shape, axis):
    return lax.broadcasted_iota(i32, shape, axis)


def plan(shard_ref, local_ref, teacher_ref, lengths_ref, table_ref, slot_ref, count_ref, mass_ref, share_ref, entropy_ref):
    group, passages = shard_ref.shape[0], lengths_ref.shape[1]
    units, padded = count_ref.shape[0], PADDED
    teacher = teacher_ref[...]
    top = jnp.max(teacher, axis=1, keepdims=True)
    log_teacher = teacher - (top + jnp.log(jnp.sum(jnp.exp(teacher - top), axis=1, keepdims=True)))
    probs = jnp.exp(log_teacher)
    here = shard_ref[...] == lax.axis_index("passage")
    entropy_ref[...] = jnp.broadcast_to(jnp.sum(jnp.where(here, probs * log_teacher, 0.0), keepdims=True), entropy_ref.shape)
    key = jnp.where(here, local_ref[...], -1)
    row = iota((passages, key.shape[1]), 0)
    lane = iota((passages, LANES), 1)
    count = jnp.zeros((passages, LANES), f32)
    mass = jnp.zeros((passages, LANES), f32)
    for q in range(group):
        hit = key[q : q + 1, :] == row
        count = jnp.where(lane == q, jnp.sum(jnp.where(hit, 1.0, 0.0), axis=1, keepdims=True), count)
        mass = jnp.where(lane == q, jnp.sum(jnp.where(hit, probs[q : q + 1, :], 0.0), axis=1, keepdims=True), mass)
    live = count > 0.0
    live_b = jnp.where(live, 1.0, 0.0).astype(bf16)
    before = jnp.where(iota((LANES, LANES), 0) < iota((LANES, LANES), 1), 1.0, 0.0).astype(bf16)
    rank = jnp.dot(live_b, before, preferred_element_type=f32)
    rank = jnp.where(live, rank, -1.0)
    named = lax.dot_general(jnp.ones((8, LANES), bf16), live_b, NT, preferred_element_type=f32)
    needed = ((named.astype(i32) + (SLOTS - 1)) // SLOTS).astype(f32)
    before_p = jnp.where(iota((passages, passages), 0) < iota((passages, passages), 1), 1.0, 0.0).astype(bf16)
    first = jnp.dot(needed.astype(bf16), before_p, preferred_element_type=f32)
    needed, first = needed[0:1, :], first[0:1, :]
    total = jnp.sum(needed, axis=1, keepdims=True)
    unit = iota((padded, passages), 0).astype(f32)
    own = (unit >= first) & (unit < first + needed)
    own_f = jnp.where(own, 1.0, 0.0)
    own_b = own_f.astype(bf16)
    passage = jnp.sum(jnp.where(own, iota((padded, passages), 1).astype(f32), 0.0), axis=1, keepdims=True)
    length = jnp.sum(jnp.where(own, lengths_ref[...].astype(f32), 0.0), axis=1, keepdims=True)
    offset = jnp.sum(jnp.where(own, unit - first, 0.0), axis=1, keepdims=True) * SLOTS
    wide = iota((padded, LANES), 1)
    used = iota((padded, LANES), 0).astype(f32) < total
    unit_rank = jnp.dot(own_b, rank.astype(bf16), preferred_element_type=f32)
    slot = jnp.where(used & (unit_rank >= 0.0), unit_rank - offset, -1.0)
    here = (slot >= 0.0) & (slot < float(SLOTS))
    slot = jnp.where(here, slot, -1.0)
    unit_count = jnp.where(here, jnp.dot(own_b, count.astype(bf16), preferred_element_type=f32), 0.0)
    unit_mass = jnp.dot(own_f, mass, preferred_element_type=f32, precision=lax.Precision.HIGHEST)
    unit_mass = jnp.where(here, unit_mass, 0.0)
    slot_ref[...] = slot[:units]
    count_ref[...] = unit_count[:units]
    mass_ref[...] = unit_mass[:units]
    ints = jnp.where(wide == SLOTS, passage, 0.0)
    eights = jnp.floor(length * 0.125) * 8.0
    ints = jnp.where(wide == SLOTS + 1, PLEN - eights, ints)
    ints = jnp.where(wide == SLOTS + 3, length - eights, ints)
    ints = jnp.where(wide == SLOTS + 2, total, ints)
    wide_f = wide.astype(f32)
    shares = jnp.zeros((units, LANES), f32)
    for k in range(SLOTS):
        pick = slot == float(k)
        query = group + jnp.sum(jnp.where(pick, wide_f - group, 0.0), axis=1, keepdims=True)
        ints = jnp.where(wide == k, query, ints)
        share = jnp.sum(jnp.where(pick, unit_mass, 0.0)[:units], axis=1, keepdims=True)
        shares = jnp.where(wide[:units] == SLOTS + k, share, shares)
    share_ref[...] = shares
    ints = jnp.transpose(ints).astype(i32)
    for k in range(SLOTS + 4):
        for half in range(padded // LANES):
            table_ref[pl.ds(k * (padded // LANES) + half, 1), :] = ints[k : k + 1, half * LANES : (half + 1) * LANES]


def field(k):
    return k * PADDED


def trips(table_ref, size):
    return (table_ref[field(SLOTS + 2)] + (size - 1)) // size


def score(
    table_ref, query_ref, passage_ref, slot_ref, count_ref, mass_ref, share_ref, entropy_ref,
    weight_ref, factor_ref, local_ref, own_ref,
    double_ref, row_ref, logits_ref, buffer_ref, scale_ref, cap_ref, turned_ref, sems,
):
    group, qlen = query_ref.shape[0], query_ref.shape[1]
    units, columns, plen = weight_ref.shape
    double_ref[:group] = query_ref[...] * 2
    double_ref[group] = jnp.zeros(double_ref.shape[1:], bf16)
    row_ref[...] = jnp.zeros(row_ref.shape, f32)
    for part in range(8):
        cap_ref[part] = jnp.where(iota((2 * plen, columns), 0) < plen + part, -FLOOR, FLOOR)
    rounds = trips(table_ref, AHEAD)

    def out(t):
        first = pl.multiple_of(t * AHEAD, AHEAD)
        return pltpu.make_async_copy(
            buffer_ref.at[pl.ds(first + AHEAD, AHEAD)], weight_ref.at[pl.ds(first, AHEAD)], sems.at[t]
        )

    def turn(u):
        tokens = [double_ref[table_ref[field(k) + u]] for k in range(SLOTS)]
        return jnp.transpose(jnp.concatenate(tokens, axis=0))

    for j in range(AHEAD):
        turned_ref[j] = turn(j)

    def some(t, carry):
        for j in range(AHEAD):
            u = t * AHEAD + j
            old = logits_ref[j]
            p = table_ref[field(SLOTS) + u]
            tokens = turned_ref[j]
            turned_ref[j] = turn(u + AHEAD)
            logits = jnp.dot(passage_ref[p], tokens, preferred_element_type=f32)
            start = pl.multiple_of(table_ref[field(SLOTS + 1) + u], 8)
            logits_ref[j] = jnp.minimum(logits, cap_ref[table_ref[field(SLOTS + 3) + u], pl.ds(start, plen), :])
            top = jnp.max(old, axis=0, keepdims=True)
            terms = jnp.exp(old - top)
            total = jnp.sum(terms, axis=0, keepdims=True)
            buffer_ref[u] = jnp.transpose((terms * (1.0 / total)).astype(bf16))
            row_ref[pl.ds(u, 1), :] = top + jnp.log(total)

        @pl.when(t > 0)
        def _():
            out(t - 1).start()

        return carry

    lax.fori_loop(0, rounds + 1, some, 0)
    same = iota((columns, LANES), 0) // qlen == iota((columns, LANES), 1)
    rows = row_ref[pl.ds(AHEAD, units), :]
    summed = jnp.dot(rows, jnp.where(same, 0.5, 0.0), preferred_element_type=f32, precision=lax.Precision.HIGHEST)
    slot, count, mass = slot_ref[...], count_ref[...], mass_ref[...]
    scores = jnp.zeros((units, LANES), f32)
    for k in range(SLOTS):
        scores = jnp.where(slot == float(k), jnp.broadcast_to(summed[:, k : k + 1], (units, LANES)), scores)
    live = slot >= 0.0
    top = jnp.max(jnp.where(live, scores, FLOOR), axis=0, keepdims=True)
    gap = jnp.where(live, scores - top, 0.0)
    student = jnp.where(live, count * jnp.exp(gap), 0.0)
    scale = share_ref[...]
    wide = iota((units, LANES), 1)
    for k in range(SLOTS):
        scale = jnp.where(wide == k, jnp.sum(jnp.where(slot == float(k), student, 0.0), axis=1, keepdims=True), scale)
    scale_ref[...] = scale
    factors = pltpu.make_async_copy(scale_ref, factor_ref, sems.at[units // AHEAD])
    factors.start()
    total = jnp.sum(student, axis=0, keepdims=True)
    lane = iota((1, LANES), 1)
    cross = jnp.sum(mass * gap, axis=0, keepdims=True) - jnp.where(lane == 0, entropy_ref[...], 0.0)
    kept = jnp.sum(mass, axis=0, keepdims=True)
    packed = jnp.where(lane < group, top, 0.0)
    for k, part in enumerate((total, cross, kept)):
        moved = pltpu.roll(jnp.broadcast_to(part, (8, LANES)), (k + 1) * group, 1)[0:1]
        packed = jnp.where(lane // group == k + 1, moved, packed)
    local_ref[...] = jnp.broadcast_to(packed, local_ref.shape)
    own_ref[...] = jnp.broadcast_to(packed, own_ref.shape)

    def finish(t, carry):
        out(t).wait()
        return carry

    lax.fori_loop(0, rounds, finish, 0)
    factors.wait()


def terms_of(table_ref, weight_ref, passage_ref, factor_ref, sums_ref, scale_ref, spread_ref, grads_ref, buffer_ref, sems):
    qlen = sums_ref.shape[1] // 2
    units = weight_ref.shape[0]
    rounds = trips(table_ref, UNROLL)
    factors = pltpu.make_async_copy(factor_ref, scale_ref, sems.at[units // UNROLL])
    factors.start()

    def into(t):
        part = pl.ds(pl.multiple_of(t * UNROLL, UNROLL), UNROLL)
        return pltpu.make_async_copy(weight_ref.at[part], buffer_ref.at[part], sems.at[t])

    def begin(t, carry):
        into(t).start()
        return carry

    lax.fori_loop(0, rounds, begin, 0)
    sums_ref[...] = jnp.zeros(sums_ref.shape, f32)
    grads_ref[...] = jnp.zeros(grads_ref.shape, f32)
    factors.wait()
    scale = scale_ref[...]
    for k in range(2 * SLOTS):
        spread_ref[k] = jnp.broadcast_to(scale[:, k : k + 1], scale.shape)

    def some(t, carry):
        @pl.when(t < rounds)
        def _():
            into(t).wait()

        for j in range(UNROLL):
            old = grads_ref[j]
            late = jnp.minimum(t, rounds - 1) * UNROLL + j
            grads_ref[j] = jnp.dot(buffer_ref[late], passage_ref[table_ref[field(SLOTS) + late]], preferred_element_type=f32)
            u = jnp.maximum(t - 1, 0) * UNROLL + j
            queries = [table_ref[field(k) + u] for k in range(SLOTS)]
            sums = [sums_ref[q] for q in queries]
            for k, q in enumerate(queries):
                part = old[k * qlen : (k + 1) * qlen]
                student, share = spread_ref[k, pl.ds(u, 1), :], spread_ref[SLOTS + k, pl.ds(u, 1), :]
                sums_ref[q] = sums[k] + jnp.concatenate([student * part, share * part], axis=0)
        return carry

    @pl.when(rounds > 0)
    def _():
        lax.fori_loop(0, rounds + 1, some, 0)


def shared(parts):
    group = LANES // 4
    total, cross, kept = (pltpu.roll(parts, LANES - (k + 1) * group, 1) for k in range(3))
    top = jnp.max(parts, axis=0, keepdims=True)
    lse = top + jnp.log(jnp.sum(total * jnp.exp(parts - top), axis=0, keepdims=True))
    return lse, cross, kept


def losses(parts_ref, loss_ref):
    shards = parts_ref.shape[0] // TOLD
    loss = jnp.zeros((1, 1), f32)
    for side in range(TOLD):
        parts = parts_ref[side * shards : (side + 1) * shards]
        lse, cross, kept = shared(parts)
        agreed = jnp.sum(cross + kept * (parts - lse), axis=0, keepdims=True)
        loss = loss - jnp.sum(jnp.where(iota((1, LANES), 1) < LANES // 4, agreed, 0.0), axis=1, keepdims=True)
    loss_ref[...] = jnp.broadcast_to(loss, loss_ref.shape)


def join(parts_ref, own_ref, sums_ref, grads_ref):
    group, qlen = grads_ref.shape[0], grads_ref.shape[1]
    shards = parts_ref.shape[0] // TOLD
    side = lax.axis_index("query") % TOLD
    lse = shared(parts_ref[pl.ds(pl.multiple_of(side * shards, 8), shards), :])[0]
    factor = jnp.where(iota((1, LANES), 1) < group, jnp.exp(own_ref[0:1, :] - lse), 0.0)
    factors = jnp.transpose(jnp.broadcast_to(factor, (LANES, LANES)))
    for q in range(group):
        grads_ref[q] = sums_ref[q, :qlen] * factors[q : q + 1, :] - sums_ref[q, qlen:]


def body(query_tokens, passage_tokens, passage_lengths, cand_shard, cand_local, teacher_scores):
    shards, groups = lax.axis_size("passage"), lax.axis_size("query")
    me = lax.axis_index("passage")
    group, cands = cand_local.shape
    qlen, dim = query_tokens.shape[1:]
    passages, plen, _ = passage_tokens.shape
    units = UNITS
    queries = lax.all_to_all(jnp.broadcast_to(query_tokens, (shards, qlen, dim)), "passage", 0, 0, tiled=True)
    lengths = lax.dynamic_slice_in_dim(passage_lengths, me * passages, passages).reshape(1, passages)
    table, slot, count, mass, share, entropy = call(
        plan,
        (
            held((2 * SLOTS * PADDED // LANES, LANES), i32),
            held((units, LANES), f32),
            held((units, LANES), f32),
            held((units, LANES), f32),
            held((units, LANES), f32),
            held((1, LANES), f32),
        ),
        [VMEM, VMEM, VMEM, VMEM],
        int(2e9),
    )(cand_shard.reshape(group, cands), cand_local, teacher_scores, lengths)
    weights, factors, local, own = call(
        score,
        (
            pltpu.HBM((units, SLOTS * qlen, plen), bf16),
            pltpu.HBM((units, LANES), f32),
            held((TOLD * shards, LANES), f32),
            held((8, LANES), f32),
        ),
        [SMEM, VMEM, VMEM, VMEM, VMEM, VMEM, VMEM, VMEM],
        int(4e9),
        [
            pltpu.VMEM((group + 1, qlen, dim), bf16),
            pltpu.VMEM((AHEAD + units, LANES), f32),
            pltpu.VMEM((AHEAD, plen, SLOTS * qlen), f32),
            pltpu.VMEM((AHEAD + units, SLOTS * qlen, plen), bf16),
            pltpu.VMEM((units, LANES), f32),
            pltpu.VMEM((8, 2 * plen, SLOTS * qlen), f32),
            pltpu.VMEM((AHEAD, dim, SLOTS * qlen), bf16),
            pltpu.SemaphoreType.DMA((units // AHEAD + 1,)),
        ],
    )(table.reshape(-1), queries, passage_tokens, slot, count, mass, share, entropy)
    told = [list(range(a, a + TOLD)) for a in range(0, groups, TOLD)]
    sets = [[g * shards + s for g in members for s in range(shards)] for members in told]
    parts = lax.all_to_all(
        local.reshape(TOLD * shards, 1, LANES), ("query", "passage"), 0, 0, tiled=True, axis_index_groups=sets
    )
    (sums,) = call(
        terms_of,
        (held((group + 1, 2 * qlen, dim), f32),),
        [SMEM, HBM, VMEM, HBM],
        int(4e9),
        [
            pltpu.VMEM((units, LANES), f32),
            pltpu.VMEM((2 * SLOTS, units, LANES), f32),
            pltpu.VMEM((UNROLL, SLOTS * qlen, dim), f32),
            pltpu.VMEM((units, SLOTS * qlen, plen), bf16),
            pltpu.SemaphoreType.DMA((units // UNROLL + 1,)),
        ],
    )(table.reshape(-1), in_hbm(weights), passage_tokens, in_hbm(factors))
    parts = parts.reshape(TOLD * shards, LANES)
    (grads,) = call(
        join, (jax.ShapeDtypeStruct((group, qlen, dim), f32),), [VMEM, VMEM, VMEM], int(1e9)
    )(parts, own, sums)
    (loss,) = call(losses, (jax.ShapeDtypeStruct((1, LANES), f32),), [VMEM], int(1e9))(parts)
    sent = lax.all_to_all(grads, "passage", 0, 0, tiled=True)
    left = [list(members) for members in zip(*told)]
    loss = lax.psum(loss, "query", axis_index_groups=left)
    query_grads = jnp.sum(sent, axis=0, keepdims=True)
    return (loss[0, 0] / (groups * group), query_grads)


def solution(mesh):
    placed = (
        P(("query", "passage"), None, None),
        P("passage", None, None),
        P(),
        P("query", None, None),
        P("query", None),
        P("query", None),
    )
    return jax.shard_map(
        body,
        mesh=mesh,
        in_specs=placed,
        out_specs=(P(), P(("query", "passage"), None, None)),
        check_vma=False,
    )
```

```python
import math
import jax
import jax.numpy as jnp
from jax import lax
from jax.experimental import pallas as pl
from jax.experimental.pallas import tpu as pltpu
from jax.sharding import PartitionSpec as P

LANES = 128
SLOTS = 4
AHEAD = 16
UNROLL = 8
UNITS = 176
PLEN = 128
PADDED = 256
TOLD = 4
FLOOR = -1e30
NT = (((1,), (1,)), ((), ()))
VMEM = pl.BlockSpec(memory_space=pltpu.VMEM)
HBM = pl.BlockSpec(memory_space=pltpu.HBM)
SMEM = pl.BlockSpec(memory_space=pltpu.SMEM)
f32 = jnp.float32
bf16 = jnp.bfloat16
i32 = jnp.int32


def held(shape, dtype):
    return pltpu.VMEM(shape, dtype)


def in_hbm(array):
    return pltpu.with_memory_space_constraint(array, pltpu.HBM)


def call(kernel, outs, in_specs, cost, scratch=()):
    return pl.pallas_call(
        kernel,
        out_shape=outs,
        in_specs=in_specs,
        out_specs=tuple(HBM if getattr(o, "memory_space", None) == pltpu.HBM else VMEM for o in outs),
        scratch_shapes=scratch,
        compiler_params=pltpu.CompilerParams(vmem_limit_bytes=24 * 1024 * 1024),
        cost_estimate=pl.CostEstimate(flops=cost, bytes_accessed=cost // 100, transcendentals=0),
    )


def iota(shape, axis):
    return lax.broadcasted_iota(i32, shape, axis)


def plan(shard_ref, local_ref, teacher_ref, lengths_ref, table_ref, slot_ref, count_ref, mass_ref, share_ref, entropy_ref):
    group, passages = shard_ref.shape[0], lengths_ref.shape[1]
    units, padded = count_ref.shape[0], PADDED
    teacher = teacher_ref[...]
    top = jnp.max(teacher, axis=1, keepdims=True)
    log_teacher = teacher - (top + jnp.log(jnp.sum(jnp.exp(teacher - top), axis=1, keepdims=True)))
    probs = jnp.exp(log_teacher)
    here = shard_ref[...] == lax.axis_index("passage")
    entropy_ref[...] = jnp.broadcast_to(jnp.sum(jnp.where(here, probs * log_teacher, 0.0), keepdims=True), entropy_ref.shape)
    key = jnp.where(here, local_ref[...], -1)
    row = iota((passages, key.shape[1]), 0)
    lane = iota((passages, LANES), 1)
    count = jnp.zeros((passages, LANES), f32)
    mass = jnp.zeros((passages, LANES), f32)
    for q in range(group):
        hit = key[q : q + 1, :] == row
        count = jnp.where(lane == q, jnp.sum(jnp.where(hit, 1.0, 0.0), axis=1, keepdims=True), count)
        mass = jnp.where(lane == q, jnp.sum(jnp.where(hit, probs[q : q + 1, :], 0.0), axis=1, keepdims=True), mass)
    live = count > 0.0
    live_b = jnp.where(live, 1.0, 0.0).astype(bf16)
    before = jnp.where(iota((LANES, LANES), 0) < iota((LANES, LANES), 1), 1.0, 0.0).astype(bf16)
    rank = jnp.dot(live_b, before, preferred_element_type=f32)
    rank = jnp.where(live, rank, -1.0)
    named = lax.dot_general(jnp.ones((8, LANES), bf16), live_b, NT, preferred_element_type=f32)
    needed = ((named.astype(i32) + (SLOTS - 1)) // SLOTS).astype(f32)
    before_p = jnp.where(iota((passages, passages), 0) < iota((passages, passages), 1), 1.0, 0.0).astype(bf16)
    first = jnp.dot(needed.astype(bf16), before_p, preferred_element_type=f32)
    needed, first = needed[0:1, :], first[0:1, :]
    total = jnp.sum(needed, axis=1, keepdims=True)
    unit = iota((padded, passages), 0).astype(f32)
    own = (unit >= first) & (unit < first + needed)
    own_f = jnp.where(own, 1.0, 0.0)
    own_b = own_f.astype(bf16)
    passage = jnp.sum(jnp.where(own, iota((padded, passages), 1).astype(f32), 0.0), axis=1, keepdims=True)
    length = jnp.sum(jnp.where(own, lengths_ref[...].astype(f32), 0.0), axis=1, keepdims=True)
    offset = jnp.sum(jnp.where(own, unit - first, 0.0), axis=1, keepdims=True) * SLOTS
    wide = iota((padded, LANES), 1)
    used = iota((padded, LANES), 0).astype(f32) < total
    unit_rank = jnp.dot(own_b, rank.astype(bf16), preferred_element_type=f32)
    slot = jnp.where(used & (unit_rank >= 0.0), unit_rank - offset, -1.0)
    here = (slot >= 0.0) & (slot < float(SLOTS))
    slot = jnp.where(here, slot, -1.0)
    unit_count = jnp.where(here, jnp.dot(own_b, count.astype(bf16), preferred_element_type=f32), 0.0)
    unit_mass = jnp.dot(own_f, mass, preferred_element_type=f32, precision=lax.Precision.HIGHEST)
    unit_mass = jnp.where(here, unit_mass, 0.0)
    slot_ref[...] = slot[:units]
    count_ref[...] = unit_count[:units]
    mass_ref[...] = unit_mass[:units]
    ints = jnp.where(wide == SLOTS, passage, 0.0)
    eights = jnp.floor(length * 0.125) * 8.0
    ints = jnp.where(wide == SLOTS + 1, PLEN - eights, ints)
    ints = jnp.where(wide == SLOTS + 3, length - eights, ints)
    ints = jnp.where(wide == SLOTS + 2, total, ints)
    wide_f = wide.astype(f32)
    shares = jnp.zeros((units, LANES), f32)
    for k in range(SLOTS):
        pick = slot == float(k)
        query = group + jnp.sum(jnp.where(pick, wide_f - group, 0.0), axis=1, keepdims=True)
        ints = jnp.where(wide == k, query, ints)
        share = jnp.sum(jnp.where(pick, unit_mass, 0.0)[:units], axis=1, keepdims=True)
        shares = jnp.where(wide[:units] == SLOTS + k, share, shares)
    share_ref[...] = shares
    ints = jnp.transpose(ints).astype(i32)
    for k in range(SLOTS + 4):
        for half in range(padded // LANES):
            table_ref[pl.ds(k * (padded // LANES) + half, 1), :] = ints[k : k + 1, half * LANES : (half + 1) * LANES]


def field(k):
    return k * PADDED


def trips(table_ref, size):
    return (table_ref[field(SLOTS + 2)] + (size - 1)) // size


def score(
    table_ref, query_ref, passage_ref, slot_ref, count_ref, mass_ref, share_ref, entropy_ref,
    weight_ref, factor_ref, local_ref, own_ref,
    double_ref, row_ref, logits_ref, buffer_ref, scale_ref, cap_ref, turned_ref, sems,
):
    group, qlen = query_ref.shape[0], query_ref.shape[1]
    units, columns, plen = weight_ref.shape
    double_ref[:group] = query_ref[...] * 2
    double_ref[group] = jnp.zeros(double_ref.shape[1:], bf16)
    row_ref[...] = jnp.zeros(row_ref.shape, f32)
    for part in range(8):
        cap_ref[part] = jnp.where(iota((2 * plen, columns), 0) < plen + part, -FLOOR, FLOOR)
    rounds = trips(table_ref, AHEAD)

    def out(t):
        first = pl.multiple_of(t * AHEAD, AHEAD)
        return pltpu.make_async_copy(
            buffer_ref.at[pl.ds(first + AHEAD, AHEAD)], weight_ref.at[pl.ds(first, AHEAD)], sems.at[t]
        )

    def turn(u):
        tokens = [double_ref[table_ref[field(k) + u]] for k in range(SLOTS)]
        return jnp.transpose(jnp.concatenate(tokens, axis=0))

    for j in range(AHEAD):
        turned_ref[j] = turn(j)

    def some(t, carry):
        for j in range(AHEAD):
            u = t * AHEAD + j
            old = logits_ref[j]
            p = table_ref[field(SLOTS) + u]
            tokens = turned_ref[j]
            turned_ref[j] = turn(u + AHEAD)
            logits = jnp.dot(passage_ref[p], tokens, preferred_element_type=f32)
            start = pl.multiple_of(table_ref[field(SLOTS + 1) + u], 8)
            logits_ref[j] = jnp.minimum(logits, cap_ref[table_ref[field(SLOTS + 3) + u], pl.ds(start, plen), :])
            top = jnp.max(old, axis=0, keepdims=True)
            terms = jnp.exp(old - top)
            total = jnp.sum(terms, axis=0, keepdims=True)
            buffer_ref[u] = jnp.transpose((terms * (1.0 / total)).astype(bf16))
            row_ref[pl.ds(u, 1), :] = top + jnp.log(total)

        @pl.when(t > 0)
        def _():
            out(t - 1).start()

        return carry

    lax.fori_loop(0, rounds + 1, some, 0)
    same = iota((columns, LANES), 0) // qlen == iota((columns, LANES), 1)
    rows = row_ref[pl.ds(AHEAD, units), :]
    summed = jnp.dot(rows, jnp.where(same, 0.5, 0.0), preferred_element_type=f32, precision=lax.Precision.HIGHEST)
    slot, count, mass = slot_ref[...], count_ref[...], mass_ref[...]
    scores = jnp.zeros((units, LANES), f32)
    for k in range(SLOTS):
        scores = jnp.where(slot == float(k), jnp.broadcast_to(summed[:, k : k + 1], (units, LANES)), scores)
    live = slot >= 0.0
    top = jnp.max(jnp.where(live, scores, FLOOR), axis=0, keepdims=True)
    gap = jnp.where(live, scores - top, 0.0)
    student = jnp.where(live, count * jnp.exp(gap), 0.0)
    scale = share_ref[...]
    wide = iota((units, LANES), 1)
    for k in range(SLOTS):
        scale = jnp.where(wide == k, jnp.sum(jnp.where(slot == float(k), student, 0.0), axis=1, keepdims=True), scale)
    scale_ref[...] = scale
    factors = pltpu.make_async_copy(scale_ref, factor_ref, sems.at[units // AHEAD])
    factors.start()
    total = jnp.sum(student, axis=0, keepdims=True)
    lane = iota((1, LANES), 1)
    cross = jnp.sum(mass * gap, axis=0, keepdims=True) - jnp.where(lane == 0, entropy_ref[...], 0.0)
    kept = jnp.sum(mass, axis=0, keepdims=True)
    packed = jnp.where(lane < group, top, 0.0)
    for k, part in enumerate((total, cross, kept)):
        moved = pltpu.roll(jnp.broadcast_to(part, (8, LANES)), (k + 1) * group, 1)[0:1]
        packed = jnp.where(lane // group == k + 1, moved, packed)
    local_ref[...] = jnp.broadcast_to(packed, local_ref.shape)
    own_ref[...] = jnp.broadcast_to(packed, own_ref.shape)

    def finish(t, carry):
        out(t).wait()
        return carry

    lax.fori_loop(0, rounds, finish, 0)
    factors.wait()


def terms_of(table_ref, weight_ref, passage_ref, factor_ref, sums_ref, scale_ref, spread_ref, grads_ref, buffer_ref, sems):
    qlen = sums_ref.shape[1] // 2
    units = weight_ref.shape[0]
    rounds = trips(table_ref, UNROLL)
    factors = pltpu.make_async_copy(factor_ref, scale_ref, sems.at[units // UNROLL])
    factors.start()

    def into(t):
        part = pl.ds(pl.multiple_of(t * UNROLL, UNROLL), UNROLL)
        return pltpu.make_async_copy(weight_ref.at[part], buffer_ref.at[part], sems.at[t])

    def begin(t, carry):
        into(t).start()
        return carry

    lax.fori_loop(0, rounds, begin, 0)
    sums_ref[...] = jnp.zeros(sums_ref.shape, f32)
    grads_ref[...] = jnp.zeros(grads_ref.shape, f32)
    factors.wait()
    scale = scale_ref[...]
    for k in range(2 * SLOTS):
        spread_ref[k] = jnp.broadcast_to(scale[:, k : k + 1], scale.shape)

    def some(t, carry):
        @pl.when(t < rounds)
        def _():
            into(t).wait()

        for j in range(UNROLL):
            old = grads_ref[j]
            late = jnp.minimum(t, rounds - 1) * UNROLL + j
            grads_ref[j] = jnp.dot(buffer_ref[late], passage_ref[table_ref[field(SLOTS) + late]], preferred_element_type=f32)
            u = jnp.maximum(t - 1, 0) * UNROLL + j
            queries = [table_ref[field(k) + u] for k in range(SLOTS)]
            sums = [sums_ref[q] for q in queries]
            for k, q in enumerate(queries):
                part = old[k * qlen : (k + 1) * qlen]
                student, share = spread_ref[k, pl.ds(u, 1), :], spread_ref[SLOTS + k, pl.ds(u, 1), :]
                sums_ref[q] = sums[k] + jnp.concatenate([student * part, share * part], axis=0)
        return carry

    @pl.when(rounds > 0)
    def _():
        lax.fori_loop(0, rounds + 1, some, 0)


def shared(parts):
    group = LANES // 4
    total, cross, kept = (pltpu.roll(parts, LANES - (k + 1) * group, 1) for k in range(3))
    top = jnp.max(parts, axis=0, keepdims=True)
    lse = top + jnp.log(jnp.sum(total * jnp.exp(parts - top), axis=0, keepdims=True))
    return lse, cross, kept


def join(parts_ref, own_ref, sums_ref, grads_ref, loss_ref):
    group, qlen = grads_ref.shape[0], grads_ref.shape[1]
    shards = parts_ref.shape[0] // TOLD
    mine = lax.axis_index("query") % TOLD
    lane = iota((1, LANES), 1)
    loss = jnp.zeros((1, 1), f32)
    lse = jnp.zeros((1, LANES), f32)
    for side in range(TOLD):
        parts = parts_ref[side * shards : (side + 1) * shards]
        found, cross, kept = shared(parts)
        agreed = jnp.sum(cross + kept * (parts - found), axis=0, keepdims=True)
        loss = loss - jnp.sum(jnp.where(lane < group, agreed, 0.0), axis=1, keepdims=True)
        lse = jnp.where(mine == side, found, lse)
    loss_ref[...] = jnp.broadcast_to(loss, loss_ref.shape)
    factor = jnp.where(lane < group, jnp.exp(own_ref[0:1, :] - lse), 0.0)
    factors = jnp.transpose(jnp.broadcast_to(factor, (LANES, LANES)))
    for q in range(group):
        grads_ref[q] = sums_ref[q, :qlen] * factors[q : q + 1, :] - sums_ref[q, qlen:]


def body(query_tokens, passage_tokens, passage_lengths, cand_shard, cand_local, teacher_scores):
    shards, groups = lax.axis_size("passage"), lax.axis_size("query")
    me = lax.axis_index("passage")
    group, cands = cand_local.shape
    qlen, dim = query_tokens.shape[1:]
    passages, plen, _ = passage_tokens.shape
    units = UNITS
    queries = lax.all_to_all(jnp.broadcast_to(query_tokens, (shards, qlen, dim)), "passage", 0, 0, tiled=True)
    lengths = lax.dynamic_slice_in_dim(passage_lengths, me * passages, passages).reshape(1, passages)
    table, slot, count, mass, share, entropy = call(
        plan,
        (
            held((2 * SLOTS * PADDED // LANES, LANES), i32),
            held((units, LANES), f32),
            held((units, LANES), f32),
            held((units, LANES), f32),
            held((units, LANES), f32),
            held((1, LANES), f32),
        ),
        [VMEM, VMEM, VMEM, VMEM],
        int(2e9),
    )(cand_shard.reshape(group, cands), cand_local, teacher_scores, lengths)
    weights, factors, local, own = call(
        score,
        (
            pltpu.HBM((units, SLOTS * qlen, plen), bf16),
            pltpu.HBM((units, LANES), f32),
            held((TOLD * shards, LANES), f32),
            held((8, LANES), f32),
        ),
        [SMEM, VMEM, VMEM, VMEM, VMEM, VMEM, VMEM, VMEM],
        int(4e9),
        [
            pltpu.VMEM((group + 1, qlen, dim), bf16),
            pltpu.VMEM((AHEAD + units, LANES), f32),
            pltpu.VMEM((AHEAD, plen, SLOTS * qlen), f32),
            pltpu.VMEM((AHEAD + units, SLOTS * qlen, plen), bf16),
            pltpu.VMEM((units, LANES), f32),
            pltpu.VMEM((8, 2 * plen, SLOTS * qlen), f32),
            pltpu.VMEM((AHEAD, dim, SLOTS * qlen), bf16),
            pltpu.SemaphoreType.DMA((units // AHEAD + 1,)),
        ],
    )(table.reshape(-1), queries, passage_tokens, slot, count, mass, share, entropy)
    told = [list(range(a, a + TOLD)) for a in range(0, groups, TOLD)]
    sets = [[g * shards + s for g in members for s in range(shards)] for members in told]
    parts = lax.all_to_all(
        local.reshape(TOLD * shards, 1, LANES), ("query", "passage"), 0, 0, tiled=True, axis_index_groups=sets
    )
    (sums,) = call(
        terms_of,
        (held((group + 1, 2 * qlen, dim), f32),),
        [SMEM, HBM, VMEM, HBM],
        int(4e9),
        [
            pltpu.VMEM((units, LANES), f32),
            pltpu.VMEM((2 * SLOTS, units, LANES), f32),
            pltpu.VMEM((UNROLL, SLOTS * qlen, dim), f32),
            pltpu.VMEM((units, SLOTS * qlen, plen), bf16),
            pltpu.SemaphoreType.DMA((units // UNROLL + 1,)),
        ],
    )(table.reshape(-1), in_hbm(weights), passage_tokens, in_hbm(factors))
    parts = parts.reshape(TOLD * shards, LANES)
    grads, loss = call(
        join,
        (jax.ShapeDtypeStruct((group, qlen, dim), f32), jax.ShapeDtypeStruct((1, LANES), f32)),
        [VMEM, VMEM, VMEM],
        int(1e9),
    )(parts, own, sums)
    sent = lax.all_to_all(grads, "passage", 0, 0, tiled=True)
    left = [list(members) for members in zip(*told)]
    loss = jnp.sum(lax.all_gather(loss, "query", axis=0, tiled=True, axis_index_groups=left), axis=0, keepdims=True)
    query_grads = jnp.sum(sent, axis=0, keepdims=True)
    return (loss[0, 0] / (groups * group), query_grads)


def solution(mesh):
    placed = (
        P(("query", "passage"), None, None),
        P("passage", None, None),
        P(),
        P("query", None, None),
        P("query", None),
        P("query", None),
    )
    return jax.shard_map(
        body,
        mesh=mesh,
        in_specs=placed,
        out_specs=(P(), P(("query", "passage"), None, None)),
        check_vma=False,
    )
```

```python
import math
import jax
import jax.numpy as jnp
from jax import lax
from jax.experimental import pallas as pl
from jax.experimental.pallas import tpu as pltpu
from jax.sharding import PartitionSpec as P

LANES = 128
SLOTS = 4
AHEAD = 16
UNROLL = 8
UNITS = 176
PLEN = 128
PADDED = 256
TOLD = 4
FLOOR = -1e30
NT = (((1,), (1,)), ((), ()))
VMEM = pl.BlockSpec(memory_space=pltpu.VMEM)
HBM = pl.BlockSpec(memory_space=pltpu.HBM)
SMEM = pl.BlockSpec(memory_space=pltpu.SMEM)
f32 = jnp.float32
bf16 = jnp.bfloat16
i32 = jnp.int32


def held(shape, dtype):
    return pltpu.VMEM(shape, dtype)


def in_hbm(array):
    return pltpu.with_memory_space_constraint(array, pltpu.HBM)


def call(kernel, outs, in_specs, cost, scratch=()):
    return pl.pallas_call(
        kernel,
        out_shape=outs,
        in_specs=in_specs,
        out_specs=tuple(HBM if getattr(o, "memory_space", None) == pltpu.HBM else VMEM for o in outs),
        scratch_shapes=scratch,
        compiler_params=pltpu.CompilerParams(vmem_limit_bytes=24 * 1024 * 1024),
        cost_estimate=pl.CostEstimate(flops=cost, bytes_accessed=cost // 100, transcendentals=0),
    )


def turns(shards):
    rows = shards // 4
    return [4 * (3 * row % rows) + column for column in range(4) for row in range(rows)]


def iota(shape, axis):
    return lax.broadcasted_iota(i32, shape, axis)


def plan(shard_ref, local_ref, teacher_ref, lengths_ref, table_ref, slot_ref, count_ref, mass_ref, share_ref, entropy_ref):
    group, passages = shard_ref.shape[0], lengths_ref.shape[1]
    units, padded = count_ref.shape[0], PADDED
    teacher = teacher_ref[...]
    top = jnp.max(teacher, axis=1, keepdims=True)
    log_teacher = teacher - (top + jnp.log(jnp.sum(jnp.exp(teacher - top), axis=1, keepdims=True)))
    probs = jnp.exp(log_teacher)
    here = shard_ref[...] == lax.axis_index("passage")
    entropy_ref[...] = jnp.broadcast_to(jnp.sum(jnp.where(here, probs * log_teacher, 0.0), keepdims=True), entropy_ref.shape)
    key = jnp.where(here, local_ref[...], -1)
    row = iota((passages, key.shape[1]), 0)
    lane = iota((passages, LANES), 1)
    count = jnp.zeros((passages, LANES), f32)
    mass = jnp.zeros((passages, LANES), f32)
    for q in range(group):
        hit = key[q : q + 1, :] == row
        count = jnp.where(lane == q, jnp.sum(jnp.where(hit, 1.0, 0.0), axis=1, keepdims=True), count)
        mass = jnp.where(lane == q, jnp.sum(jnp.where(hit, probs[q : q + 1, :], 0.0), axis=1, keepdims=True), mass)
    live = count > 0.0
    live_b = jnp.where(live, 1.0, 0.0).astype(bf16)
    before = jnp.where(iota((LANES, LANES), 0) < iota((LANES, LANES), 1), 1.0, 0.0).astype(bf16)
    rank = jnp.dot(live_b, before, preferred_element_type=f32)
    rank = jnp.where(live, rank, -1.0)
    named = lax.dot_general(jnp.ones((8, LANES), bf16), live_b, NT, preferred_element_type=f32)
    needed = ((named.astype(i32) + (SLOTS - 1)) // SLOTS).astype(f32)
    before_p = jnp.where(iota((passages, passages), 0) < iota((passages, passages), 1), 1.0, 0.0).astype(bf16)
    first = jnp.dot(needed.astype(bf16), before_p, preferred_element_type=f32)
    needed, first = needed[0:1, :], first[0:1, :]
    total = jnp.sum(needed, axis=1, keepdims=True)
    unit = iota((padded, passages), 0).astype(f32)
    own = (unit >= first) & (unit < first + needed)
    own_f = jnp.where(own, 1.0, 0.0)
    own_b = own_f.astype(bf16)
    passage = jnp.sum(jnp.where(own, iota((padded, passages), 1).astype(f32), 0.0), axis=1, keepdims=True)
    length = jnp.sum(jnp.where(own, lengths_ref[...].astype(f32), 0.0), axis=1, keepdims=True)
    offset = jnp.sum(jnp.where(own, unit - first, 0.0), axis=1, keepdims=True) * SLOTS
    wide = iota((padded, LANES), 1)
    used = iota((padded, LANES), 0).astype(f32) < total
    unit_rank = jnp.dot(own_b, rank.astype(bf16), preferred_element_type=f32)
    slot = jnp.where(used & (unit_rank >= 0.0), unit_rank - offset, -1.0)
    here = (slot >= 0.0) & (slot < float(SLOTS))
    slot = jnp.where(here, slot, -1.0)
    unit_count = jnp.where(here, jnp.dot(own_b, count.astype(bf16), preferred_element_type=f32), 0.0)
    unit_mass = jnp.dot(own_f, mass, preferred_element_type=f32, precision=lax.Precision.HIGHEST)
    unit_mass = jnp.where(here, unit_mass, 0.0)
    slot_ref[...] = slot[:units]
    count_ref[...] = unit_count[:units]
    mass_ref[...] = unit_mass[:units]
    ints = jnp.where(wide == SLOTS, passage, 0.0)
    eights = jnp.floor(length * 0.125) * 8.0
    ints = jnp.where(wide == SLOTS + 1, PLEN - eights, ints)
    ints = jnp.where(wide == SLOTS + 3, length - eights, ints)
    ints = jnp.where(wide == SLOTS + 2, total, ints)
    wide_f = wide.astype(f32)
    shares = jnp.zeros((units, LANES), f32)
    for k in range(SLOTS):
        pick = slot == float(k)
        query = group + jnp.sum(jnp.where(pick, wide_f - group, 0.0), axis=1, keepdims=True)
        ints = jnp.where(wide == k, query, ints)
        share = jnp.sum(jnp.where(pick, unit_mass, 0.0)[:units], axis=1, keepdims=True)
        shares = jnp.where(wide[:units] == SLOTS + k, share, shares)
    share_ref[...] = shares
    ints = jnp.transpose(ints).astype(i32)
    for k in range(SLOTS + 4):
        for half in range(padded // LANES):
            table_ref[pl.ds(k * (padded // LANES) + half, 1), :] = ints[k : k + 1, half * LANES : (half + 1) * LANES]


def field(k):
    return k * PADDED


def trips(table_ref, size):
    return (table_ref[field(SLOTS + 2)] + (size - 1)) // size


def score(
    table_ref, query_ref, passage_ref, slot_ref, count_ref, mass_ref, share_ref, entropy_ref,
    weight_ref, factor_ref, local_ref, own_ref,
    double_ref, row_ref, logits_ref, buffer_ref, scale_ref, cap_ref, turned_ref, sems,
):
    group, qlen = query_ref.shape[0], query_ref.shape[1]
    units, columns, plen = weight_ref.shape
    double_ref[:group] = query_ref[...] * 2
    double_ref[group] = jnp.zeros(double_ref.shape[1:], bf16)
    row_ref[...] = jnp.zeros(row_ref.shape, f32)
    for part in range(8):
        cap_ref[part] = jnp.where(iota((2 * plen, columns), 0) < plen + part, -FLOOR, FLOOR)
    rounds = trips(table_ref, AHEAD)

    def out(t):
        first = pl.multiple_of(t * AHEAD, AHEAD)
        return pltpu.make_async_copy(
            buffer_ref.at[pl.ds(first + AHEAD, AHEAD)], weight_ref.at[pl.ds(first, AHEAD)], sems.at[t]
        )

    def turn(u):
        tokens = [double_ref[table_ref[field(k) + u]] for k in range(SLOTS)]
        return jnp.transpose(jnp.concatenate(tokens, axis=0))

    for j in range(AHEAD):
        turned_ref[j] = turn(j)

    def some(t, carry):
        for j in range(AHEAD):
            u = t * AHEAD + j
            old = logits_ref[j]
            p = table_ref[field(SLOTS) + u]
            tokens = turned_ref[j]
            turned_ref[j] = turn(u + AHEAD)
            logits = jnp.dot(passage_ref[p], tokens, preferred_element_type=f32)
            start = pl.multiple_of(table_ref[field(SLOTS + 1) + u], 8)
            logits_ref[j] = jnp.minimum(logits, cap_ref[table_ref[field(SLOTS + 3) + u], pl.ds(start, plen), :])
            top = jnp.max(old, axis=0, keepdims=True)
            terms = jnp.exp(old - top)
            total = jnp.sum(terms, axis=0, keepdims=True)
            buffer_ref[u] = jnp.transpose((terms * (1.0 / total)).astype(bf16))
            row_ref[pl.ds(u, 1), :] = top + jnp.log(total)

        @pl.when(t > 0)
        def _():
            out(t - 1).start()

        return carry

    lax.fori_loop(0, rounds + 1, some, 0)
    same = iota((columns, LANES), 0) // qlen == iota((columns, LANES), 1)
    rows = row_ref[pl.ds(AHEAD, units), :]
    summed = jnp.dot(rows, jnp.where(same, 0.5, 0.0), preferred_element_type=f32, precision=lax.Precision.HIGHEST)
    slot, count, mass = slot_ref[...], count_ref[...], mass_ref[...]
    scores = jnp.zeros((units, LANES), f32)
    for k in range(SLOTS):
        scores = jnp.where(slot == float(k), jnp.broadcast_to(summed[:, k : k + 1], (units, LANES)), scores)
    live = slot >= 0.0
    top = jnp.max(jnp.where(live, scores, FLOOR), axis=0, keepdims=True)
    gap = jnp.where(live, scores - top, 0.0)
    student = jnp.where(live, count * jnp.exp(gap), 0.0)
    scale = share_ref[...]
    wide = iota((units, LANES), 1)
    for k in range(SLOTS):
        scale = jnp.where(wide == k, jnp.sum(jnp.where(slot == float(k), student, 0.0), axis=1, keepdims=True), scale)
    scale_ref[...] = scale
    factors = pltpu.make_async_copy(scale_ref, factor_ref, sems.at[units // AHEAD])
    factors.start()
    total = jnp.sum(student, axis=0, keepdims=True)
    lane = iota((1, LANES), 1)
    cross = jnp.sum(mass * gap, axis=0, keepdims=True) - jnp.where(lane == 0, entropy_ref[...], 0.0)
    kept = jnp.sum(mass, axis=0, keepdims=True)
    packed = jnp.where(lane < group, top, 0.0)
    for k, part in enumerate((total, cross, kept)):
        moved = pltpu.roll(jnp.broadcast_to(part, (8, LANES)), (k + 1) * group, 1)[0:1]
        packed = jnp.where(lane // group == k + 1, moved, packed)
    local_ref[...] = jnp.broadcast_to(packed, local_ref.shape)
    own_ref[...] = jnp.broadcast_to(packed, own_ref.shape)

    def finish(t, carry):
        out(t).wait()
        return carry

    lax.fori_loop(0, rounds, finish, 0)
    factors.wait()


def terms_of(table_ref, weight_ref, passage_ref, factor_ref, sums_ref, scale_ref, spread_ref, grads_ref, buffer_ref, sems):
    qlen = sums_ref.shape[1] // 2
    units = weight_ref.shape[0]
    rounds = trips(table_ref, UNROLL)
    factors = pltpu.make_async_copy(factor_ref, scale_ref, sems.at[units // UNROLL])
    factors.start()

    def into(t):
        part = pl.ds(pl.multiple_of(t * UNROLL, UNROLL), UNROLL)
        return pltpu.make_async_copy(weight_ref.at[part], buffer_ref.at[part], sems.at[t])

    def begin(t, carry):
        into(t).start()
        return carry

    lax.fori_loop(0, rounds, begin, 0)
    sums_ref[...] = jnp.zeros(sums_ref.shape, f32)
    grads_ref[...] = jnp.zeros(grads_ref.shape, f32)
    factors.wait()
    scale = scale_ref[...]
    for k in range(2 * SLOTS):
        spread_ref[k] = jnp.broadcast_to(scale[:, k : k + 1], scale.shape)

    def some(t, carry):
        @pl.when(t < rounds)
        def _():
            into(t).wait()

        for j in range(UNROLL):
            old = grads_ref[j]
            late = jnp.minimum(t, rounds - 1) * UNROLL + j
            grads_ref[j] = jnp.dot(buffer_ref[late], passage_ref[table_ref[field(SLOTS) + late]], preferred_element_type=f32)
            u = jnp.maximum(t - 1, 0) * UNROLL + j
            queries = [table_ref[field(k) + u] for k in range(SLOTS)]
            sums = [sums_ref[q] for q in queries]
            for k, q in enumerate(queries):
                part = old[k * qlen : (k + 1) * qlen]
                student, share = spread_ref[k, pl.ds(u, 1), :], spread_ref[SLOTS + k, pl.ds(u, 1), :]
                sums_ref[q] = sums[k] + jnp.concatenate([student * part, share * part], axis=0)
        return carry

    @pl.when(rounds > 0)
    def _():
        lax.fori_loop(0, rounds + 1, some, 0)


def shared(parts):
    group = LANES // 4
    total, cross, kept = (pltpu.roll(parts, LANES - (k + 1) * group, 1) for k in range(3))
    top = jnp.max(parts, axis=0, keepdims=True)
    lse = top + jnp.log(jnp.sum(total * jnp.exp(parts - top), axis=0, keepdims=True))
    return lse, cross, kept


def join(parts_ref, own_ref, sums_ref, grads_ref, loss_ref):
    group, qlen = grads_ref.shape[0], grads_ref.shape[1]
    shards = parts_ref.shape[0] // TOLD
    mine = lax.axis_index("query") % TOLD
    lane = iota((1, LANES), 1)
    loss = jnp.zeros((1, 1), f32)
    lse = jnp.zeros((1, LANES), f32)
    for side in range(TOLD):
        parts = parts_ref[side * shards : (side + 1) * shards]
        found, cross, kept = shared(parts)
        agreed = jnp.sum(cross + kept * (parts - found), axis=0, keepdims=True)
        loss = loss - jnp.sum(jnp.where(lane < group, agreed, 0.0), axis=1, keepdims=True)
        lse = jnp.where(mine == side, found, lse)
    loss_ref[...] = jnp.broadcast_to(loss, loss_ref.shape)
    factor = jnp.where(lane < group, jnp.exp(own_ref[0:1, :] - lse), 0.0)
    factors = jnp.transpose(jnp.broadcast_to(factor, (LANES, LANES)))
    for place, q in enumerate(turns(group)):
        grads_ref[place] = sums_ref[q, :qlen] * factors[q : q + 1, :] - sums_ref[q, qlen:]


def body(query_tokens, passage_tokens, passage_lengths, cand_shard, cand_local, teacher_scores):
    shards, groups = lax.axis_size("passage"), lax.axis_size("query")
    me = lax.axis_index("passage")
    group, cands = cand_local.shape
    qlen, dim = query_tokens.shape[1:]
    passages, plen, _ = passage_tokens.shape
    units = UNITS
    queries = lax.all_to_all(jnp.broadcast_to(query_tokens, (shards, qlen, dim)), "passage", 0, 0, tiled=True)
    lengths = lax.dynamic_slice_in_dim(passage_lengths, me * passages, passages).reshape(1, passages)
    table, slot, count, mass, share, entropy = call(
        plan,
        (
            held((2 * SLOTS * PADDED // LANES, LANES), i32),
            held((units, LANES), f32),
            held((units, LANES), f32),
            held((units, LANES), f32),
            held((units, LANES), f32),
            held((1, LANES), f32),
        ),
        [VMEM, VMEM, VMEM, VMEM],
        int(2e9),
    )(cand_shard.reshape(group, cands), cand_local, teacher_scores, lengths)
    weights, factors, local, own = call(
        score,
        (
            pltpu.HBM((units, SLOTS * qlen, plen), bf16),
            pltpu.HBM((units, LANES), f32),
            held((TOLD * shards, LANES), f32),
            held((8, LANES), f32),
        ),
        [SMEM, VMEM, VMEM, VMEM, VMEM, VMEM, VMEM, VMEM],
        int(4e9),
        [
            pltpu.VMEM((group + 1, qlen, dim), bf16),
            pltpu.VMEM((AHEAD + units, LANES), f32),
            pltpu.VMEM((AHEAD, plen, SLOTS * qlen), f32),
            pltpu.VMEM((AHEAD + units, SLOTS * qlen, plen), bf16),
            pltpu.VMEM((units, LANES), f32),
            pltpu.VMEM((8, 2 * plen, SLOTS * qlen), f32),
            pltpu.VMEM((AHEAD, dim, SLOTS * qlen), bf16),
            pltpu.SemaphoreType.DMA((units // AHEAD + 1,)),
        ],
    )(table.reshape(-1), queries, passage_tokens, slot, count, mass, share, entropy)
    told = [list(range(a, a + TOLD)) for a in range(0, groups, TOLD)]
    sets = [[g * shards + s for g in members for s in range(shards)] for members in told]
    parts = lax.all_to_all(
        local.reshape(TOLD * shards, 1, LANES), ("query", "passage"), 0, 0, tiled=True, axis_index_groups=sets
    )
    (sums,) = call(
        terms_of,
        (held((group + 1, 2 * qlen, dim), f32),),
        [SMEM, HBM, VMEM, HBM],
        int(4e9),
        [
            pltpu.VMEM((units, LANES), f32),
            pltpu.VMEM((2 * SLOTS, units, LANES), f32),
            pltpu.VMEM((UNROLL, SLOTS * qlen, dim), f32),
            pltpu.VMEM((units, SLOTS * qlen, plen), bf16),
            pltpu.SemaphoreType.DMA((units // UNROLL + 1,)),
        ],
    )(table.reshape(-1), in_hbm(weights), passage_tokens, in_hbm(factors))
    parts = parts.reshape(TOLD * shards, LANES)
    grads, loss = call(
        join,
        (jax.ShapeDtypeStruct((group, qlen, dim), f32), jax.ShapeDtypeStruct((1, LANES), f32)),
        [VMEM, VMEM, VMEM],
        int(1e9),
    )(parts, own, sums)
    sent = lax.all_to_all(grads, "passage", 0, 0, tiled=True, axis_index_groups=[turns(shards)])
    left = [list(members) for members in zip(*told)]
    loss = jnp.sum(lax.all_gather(loss, "query", axis=0, tiled=True, axis_index_groups=left), axis=0, keepdims=True)
    query_grads = jnp.sum(sent, axis=0, keepdims=True)
    return (loss[0, 0] / (groups * group), query_grads)


def solution(mesh):
    placed = (
        P(("query", "passage"), None, None),
        P("passage", None, None),
        P(),
        P("query", None, None),
        P("query", None),
        P("query", None),
    )
    return jax.shard_map(
        body,
        mesh=mesh,
        in_specs=placed,
        out_specs=(P(), P(("query", "passage"), None, None)),
        check_vma=False,
    )
```

```python
import math
import jax
import jax.numpy as jnp
from jax import lax
from jax.experimental import pallas as pl
from jax.experimental.pallas import tpu as pltpu
from jax.sharding import PartitionSpec as P

LANES = 128
SLOTS = 4
AHEAD = 16
UNROLL = 8
UNITS = 176
PLEN = 128
PADDED = 256
TOLD = 4
FLOOR = -1e30
NT = (((1,), (1,)), ((), ()))
VMEM = pl.BlockSpec(memory_space=pltpu.VMEM)
HBM = pl.BlockSpec(memory_space=pltpu.HBM)
SMEM = pl.BlockSpec(memory_space=pltpu.SMEM)
f32 = jnp.float32
bf16 = jnp.bfloat16
i32 = jnp.int32


def held(shape, dtype):
    return pltpu.VMEM(shape, dtype)


def in_hbm(array):
    return pltpu.with_memory_space_constraint(array, pltpu.HBM)


def call(kernel, outs, in_specs, cost, scratch=()):
    return pl.pallas_call(
        kernel,
        out_shape=outs,
        in_specs=in_specs,
        out_specs=tuple(HBM if getattr(o, "memory_space", None) == pltpu.HBM else VMEM for o in outs),
        scratch_shapes=scratch,
        compiler_params=pltpu.CompilerParams(vmem_limit_bytes=24 * 1024 * 1024),
        cost_estimate=pl.CostEstimate(flops=cost, bytes_accessed=cost // 100, transcendentals=0),
    )


def iota(shape, axis):
    return lax.broadcasted_iota(i32, shape, axis)


def plan(shard_ref, local_ref, teacher_ref, lengths_ref, table_ref, slot_ref, count_ref, mass_ref, share_ref, entropy_ref):
    group, passages = shard_ref.shape[0], lengths_ref.shape[1]
    units, padded = count_ref.shape[0], PADDED
    teacher = teacher_ref[...]
    top = jnp.max(teacher, axis=1, keepdims=True)
    log_teacher = teacher - (top + jnp.log(jnp.sum(jnp.exp(teacher - top), axis=1, keepdims=True)))
    probs = jnp.exp(log_teacher)
    here = shard_ref[...] == lax.axis_index("passage")
    entropy_ref[...] = jnp.broadcast_to(jnp.sum(jnp.where(here, probs * log_teacher, 0.0), keepdims=True), entropy_ref.shape)
    key = jnp.where(here, local_ref[...], -1)
    row = iota((passages, key.shape[1]), 0)
    lane = iota((passages, LANES), 1)
    count = jnp.zeros((passages, LANES), f32)
    mass = jnp.zeros((passages, LANES), f32)
    for q in range(group):
        hit = key[q : q + 1, :] == row
        count = jnp.where(lane == q, jnp.sum(jnp.where(hit, 1.0, 0.0), axis=1, keepdims=True), count)
        mass = jnp.where(lane == q, jnp.sum(jnp.where(hit, probs[q : q + 1, :], 0.0), axis=1, keepdims=True), mass)
    live = count > 0.0
    live_b = jnp.where(live, 1.0, 0.0).astype(bf16)
    before = jnp.where(iota((LANES, LANES), 0) < iota((LANES, LANES), 1), 1.0, 0.0).astype(bf16)
    rank = jnp.dot(live_b, before, preferred_element_type=f32)
    rank = jnp.where(live, rank, -1.0)
    named = lax.dot_general(jnp.ones((8, LANES), bf16), live_b, NT, preferred_element_type=f32)
    needed = ((named.astype(i32) + (SLOTS - 1)) // SLOTS).astype(f32)
    before_p = jnp.where(iota((passages, passages), 0) < iota((passages, passages), 1), 1.0, 0.0).astype(bf16)
    first = jnp.dot(needed.astype(bf16), before_p, preferred_element_type=f32)
    needed, first = needed[0:1, :], first[0:1, :]
    total = jnp.sum(needed, axis=1, keepdims=True)
    unit = iota((padded, passages), 0).astype(f32)
    own = (unit >= first) & (unit < first + needed)
    own_f = jnp.where(own, 1.0, 0.0)
    own_b = own_f.astype(bf16)
    passage = jnp.sum(jnp.where(own, iota((padded, passages), 1).astype(f32), 0.0), axis=1, keepdims=True)
    length = jnp.sum(jnp.where(own, lengths_ref[...].astype(f32), 0.0), axis=1, keepdims=True)
    offset = jnp.sum(jnp.where(own, unit - first, 0.0), axis=1, keepdims=True) * SLOTS
    wide = iota((padded, LANES), 1)
    used = iota((padded, LANES), 0).astype(f32) < total
    unit_rank = jnp.dot(own_b, rank.astype(bf16), preferred_element_type=f32)
    slot = jnp.where(used & (unit_rank >= 0.0), unit_rank - offset, -1.0)
    here = (slot >= 0.0) & (slot < float(SLOTS))
    slot = jnp.where(here, slot, -1.0)
    unit_count = jnp.where(here, jnp.dot(own_b, count.astype(bf16), preferred_element_type=f32), 0.0)
    unit_mass = jnp.dot(own_f, mass, preferred_element_type=f32, precision=lax.Precision.HIGHEST)
    unit_mass = jnp.where(here, unit_mass, 0.0)
    slot_ref[...] = slot[:units]
    count_ref[...] = unit_count[:units]
    mass_ref[...] = unit_mass[:units]
    ints = jnp.where(wide == SLOTS, passage, 0.0)
    eights = jnp.floor(length * 0.125) * 8.0
    ints = jnp.where(wide == SLOTS + 1, PLEN - eights, ints)
    ints = jnp.where(wide == SLOTS + 3, length - eights, ints)
    ints = jnp.where(wide == SLOTS + 2, total, ints)
    wide_f = wide.astype(f32)
    shares = jnp.zeros((units, LANES), f32)
    for k in range(SLOTS):
        pick = slot == float(k)
        query = group + jnp.sum(jnp.where(pick, wide_f - group, 0.0), axis=1, keepdims=True)
        ints = jnp.where(wide == k, query, ints)
        share = jnp.sum(jnp.where(pick, unit_mass, 0.0)[:units], axis=1, keepdims=True)
        shares = jnp.where(wide[:units] == SLOTS + k, share, shares)
    share_ref[...] = shares
    ints = jnp.transpose(ints).astype(i32)
    for k in range(SLOTS + 4):
        for half in range(padded // LANES):
            table_ref[pl.ds(k * (padded // LANES) + half, 1), :] = ints[k : k + 1, half * LANES : (half + 1) * LANES]


def field(k):
    return k * PADDED


def trips(table_ref, size):
    return (table_ref[field(SLOTS + 2)] + (size - 1)) // size


def score(
    table_ref, query_ref, passage_ref, slot_ref, count_ref, mass_ref, share_ref, entropy_ref,
    weight_ref, factor_ref, local_ref, own_ref,
    double_ref, row_ref, logits_ref, buffer_ref, scale_ref, cap_ref, turned_ref, sems,
):
    group, qlen = query_ref.shape[0], query_ref.shape[1]
    units, columns, plen = weight_ref.shape
    double_ref[:group] = query_ref[...] * 2
    double_ref[group] = jnp.zeros(double_ref.shape[1:], bf16)
    row_ref[...] = jnp.zeros(row_ref.shape, f32)
    for part in range(8):
        cap_ref[part] = jnp.where(iota((2 * plen, columns), 0) < plen + part, -FLOOR, FLOOR)
    rounds = trips(table_ref, AHEAD)

    def out(t):
        first = pl.multiple_of(t * AHEAD, AHEAD)
        return pltpu.make_async_copy(
            buffer_ref.at[pl.ds(first + AHEAD, AHEAD)], weight_ref.at[pl.ds(first, AHEAD)], sems.at[t]
        )

    def turn(u):
        tokens = [double_ref[table_ref[field(k) + u]] for k in range(SLOTS)]
        return jnp.transpose(jnp.concatenate(tokens, axis=0))

    for j in range(AHEAD):
        turned_ref[j] = turn(j)

    def some(t, carry):
        for j in range(AHEAD):
            u = t * AHEAD + j
            old = logits_ref[j]
            p = table_ref[field(SLOTS) + u]
            tokens = turned_ref[j]
            turned_ref[j] = turn(u + AHEAD)
            logits = jnp.dot(passage_ref[p], tokens, preferred_element_type=f32)
            start = pl.multiple_of(table_ref[field(SLOTS + 1) + u], 8)
            logits_ref[j] = jnp.minimum(logits, cap_ref[table_ref[field(SLOTS + 3) + u], pl.ds(start, plen), :])
            top = jnp.max(old, axis=0, keepdims=True)
            terms = jnp.exp(old - top)
            total = jnp.sum(terms, axis=0, keepdims=True)
            buffer_ref[u] = jnp.transpose((terms * (1.0 / total)).astype(bf16))
            row_ref[pl.ds(u, 1), :] = top + jnp.log(total)

        @pl.when(t > 0)
        def _():
            out(t - 1).start()

        return carry

    lax.fori_loop(0, rounds + 1, some, 0)
    same = iota((columns, LANES), 0) // qlen == iota((columns, LANES), 1)
    rows = row_ref[pl.ds(AHEAD, units), :]
    halves = jnp.where(same, 0.5, 0.0).astype(bf16)
    summed = jnp.zeros((units, LANES), f32)
    for _ in range(3):
        part = rows.astype(bf16)
        summed += jnp.dot(part, halves, preferred_element_type=f32)
        rows -= part.astype(f32)
    slot, count, mass = slot_ref[...], count_ref[...], mass_ref[...]
    scores = jnp.zeros((units, LANES), f32)
    for k in range(SLOTS):
        scores = jnp.where(slot == float(k), jnp.broadcast_to(summed[:, k : k + 1], (units, LANES)), scores)
    live = slot >= 0.0
    top = jnp.max(jnp.where(live, scores, FLOOR), axis=0, keepdims=True)
    gap = jnp.where(live, scores - top, 0.0)
    student = jnp.where(live, count * jnp.exp(gap), 0.0)
    scale = share_ref[...]
    wide = iota((units, LANES), 1)
    for k in range(SLOTS):
        scale = jnp.where(wide == k, jnp.sum(jnp.where(slot == float(k), student, 0.0), axis=1, keepdims=True), scale)
    scale_ref[...] = scale
    factors = pltpu.make_async_copy(scale_ref, factor_ref, sems.at[units // AHEAD])
    factors.start()
    total = jnp.sum(student, axis=0, keepdims=True)
    lane = iota((1, LANES), 1)
    cross = jnp.sum(mass * gap, axis=0, keepdims=True) - jnp.where(lane == 0, entropy_ref[...], 0.0)
    kept = jnp.sum(mass, axis=0, keepdims=True)
    packed = jnp.where(lane < group, top, 0.0)
    for k, part in enumerate((total, cross, kept)):
        moved = pltpu.roll(jnp.broadcast_to(part, (8, LANES)), (k + 1) * group, 1)[0:1]
        packed = jnp.where(lane // group == k + 1, moved, packed)
    local_ref[...] = jnp.broadcast_to(packed, local_ref.shape)
    own_ref[...] = jnp.broadcast_to(packed, own_ref.shape)

    def finish(t, carry):
        out(t).wait()
        return carry

    lax.fori_loop(0, rounds, finish, 0)
    factors.wait()


def terms_of(table_ref, weight_ref, passage_ref, factor_ref, sums_ref, scale_ref, spread_ref, grads_ref, buffer_ref, sems):
    qlen = sums_ref.shape[1] // 2
    units = weight_ref.shape[0]
    rounds = trips(table_ref, UNROLL)
    factors = pltpu.make_async_copy(factor_ref, scale_ref, sems.at[units // UNROLL])
    factors.start()

    def into(t):
        part = pl.ds(pl.multiple_of(t * UNROLL, UNROLL), UNROLL)
        return pltpu.make_async_copy(weight_ref.at[part], buffer_ref.at[part], sems.at[t])

    def begin(t, carry):
        into(t).start()
        return carry

    lax.fori_loop(0, rounds, begin, 0)
    sums_ref[...] = jnp.zeros(sums_ref.shape, f32)
    grads_ref[...] = jnp.zeros(grads_ref.shape, f32)
    factors.wait()
    scale = scale_ref[...]
    for k in range(2 * SLOTS):
        spread_ref[k] = jnp.broadcast_to(scale[:, k : k + 1], scale.shape)

    def some(t, carry):
        @pl.when(t < rounds)
        def _():
            into(t).wait()

        for j in range(UNROLL):
            old = grads_ref[j]
            late = jnp.minimum(t, rounds - 1) * UNROLL + j
            grads_ref[j] = jnp.dot(buffer_ref[late], passage_ref[table_ref[field(SLOTS) + late]], preferred_element_type=f32)
            u = jnp.maximum(t - 1, 0) * UNROLL + j
            queries = [table_ref[field(k) + u] for k in range(SLOTS)]
            sums = [sums_ref[q] for q in queries]
            for k, q in enumerate(queries):
                part = old[k * qlen : (k + 1) * qlen]
                student, share = spread_ref[k, pl.ds(u, 1), :], spread_ref[SLOTS + k, pl.ds(u, 1), :]
                sums_ref[q] = sums[k] + jnp.concatenate([student * part, share * part], axis=0)
        return carry

    @pl.when(rounds > 0)
    def _():
        lax.fori_loop(0, rounds + 1, some, 0)


def shared(parts):
    group = LANES // 4
    total, cross, kept = (pltpu.roll(parts, LANES - (k + 1) * group, 1) for k in range(3))
    top = jnp.max(parts, axis=0, keepdims=True)
    lse = top + jnp.log(jnp.sum(total * jnp.exp(parts - top), axis=0, keepdims=True))
    return lse, cross, kept


def join(parts_ref, own_ref, sums_ref, grads_ref, loss_ref):
    group, qlen = grads_ref.shape[0], grads_ref.shape[1]
    shards = parts_ref.shape[0] // TOLD
    mine = lax.axis_index("query") % TOLD
    lane = iota((1, LANES), 1)
    loss = jnp.zeros((1, 1), f32)
    lse = jnp.zeros((1, LANES), f32)
    for side in range(TOLD):
        parts = parts_ref[side * shards : (side + 1) * shards]
        found, cross, kept = shared(parts)
        agreed = jnp.sum(cross + kept * (parts - found), axis=0, keepdims=True)
        loss = loss - jnp.sum(jnp.where(lane < group, agreed, 0.0), axis=1, keepdims=True)
        lse = jnp.where(mine == side, found, lse)
    loss_ref[...] = jnp.broadcast_to(loss, loss_ref.shape)
    factor = jnp.where(lane < group, jnp.exp(own_ref[0:1, :] - lse), 0.0)
    factors = jnp.transpose(jnp.broadcast_to(factor, (LANES, LANES)))
    for q in range(group):
        grads_ref[q] = sums_ref[q, :qlen] * factors[q : q + 1, :] - sums_ref[q, qlen:]


def body(query_tokens, passage_tokens, passage_lengths, cand_shard, cand_local, teacher_scores):
    shards, groups = lax.axis_size("passage"), lax.axis_size("query")
    me = lax.axis_index("passage")
    group, cands = cand_local.shape
    qlen, dim = query_tokens.shape[1:]
    passages, plen, _ = passage_tokens.shape
    units = UNITS
    queries = lax.all_to_all(jnp.broadcast_to(query_tokens, (shards, qlen, dim)), "passage", 0, 0, tiled=True)
    lengths = lax.dynamic_slice_in_dim(passage_lengths, me * passages, passages).reshape(1, passages)
    table, slot, count, mass, share, entropy = call(
        plan,
        (
            held((2 * SLOTS * PADDED // LANES, LANES), i32),
            held((units, LANES), f32),
            held((units, LANES), f32),
            held((units, LANES), f32),
            held((units, LANES), f32),
            held((1, LANES), f32),
        ),
        [VMEM, VMEM, VMEM, VMEM],
        int(2e9),
    )(cand_shard.reshape(group, cands), cand_local, teacher_scores, lengths)
    weights, factors, local, own = call(
        score,
        (
            pltpu.HBM((units, SLOTS * qlen, plen), bf16),
            pltpu.HBM((units, LANES), f32),
            held((TOLD * shards, LANES), f32),
            held((8, LANES), f32),
        ),
        [SMEM, VMEM, VMEM, VMEM, VMEM, VMEM, VMEM, VMEM],
        int(4e9),
        [
            pltpu.VMEM((group + 1, qlen, dim), bf16),
            pltpu.VMEM((AHEAD + units, LANES), f32),
            pltpu.VMEM((AHEAD, plen, SLOTS * qlen), f32),
            pltpu.VMEM((AHEAD + units, SLOTS * qlen, plen), bf16),
            pltpu.VMEM((units, LANES), f32),
            pltpu.VMEM((8, 2 * plen, SLOTS * qlen), f32),
            pltpu.VMEM((AHEAD, dim, SLOTS * qlen), bf16),
            pltpu.SemaphoreType.DMA((units // AHEAD + 1,)),
        ],
    )(table.reshape(-1), queries, passage_tokens, slot, count, mass, share, entropy)
    told = [list(range(a, a + TOLD)) for a in range(0, groups, TOLD)]
    sets = [[g * shards + s for g in members for s in range(shards)] for members in told]
    parts = lax.all_to_all(
        local.reshape(TOLD * shards, 1, LANES), ("query", "passage"), 0, 0, tiled=True, axis_index_groups=sets
    )
    (sums,) = call(
        terms_of,
        (held((group + 1, 2 * qlen, dim), f32),),
        [SMEM, HBM, VMEM, HBM],
        int(4e9),
        [
            pltpu.VMEM((units, LANES), f32),
            pltpu.VMEM((2 * SLOTS, units, LANES), f32),
            pltpu.VMEM((UNROLL, SLOTS * qlen, dim), f32),
            pltpu.VMEM((units, SLOTS * qlen, plen), bf16),
            pltpu.SemaphoreType.DMA((units // UNROLL + 1,)),
        ],
    )(table.reshape(-1), in_hbm(weights), passage_tokens, in_hbm(factors))
    parts = parts.reshape(TOLD * shards, LANES)
    grads, loss = call(
        join,
        (jax.ShapeDtypeStruct((group, qlen, dim), f32), jax.ShapeDtypeStruct((1, LANES), f32)),
        [VMEM, VMEM, VMEM],
        int(1e9),
    )(parts, own, sums)
    sent = lax.all_to_all(grads, "passage", 0, 0, tiled=True)
    left = [list(members) for members in zip(*told)]
    loss = jnp.sum(lax.all_gather(loss, "query", axis=0, tiled=True, axis_index_groups=left), axis=0, keepdims=True)
    query_grads = jnp.sum(sent, axis=0, keepdims=True)
    return (loss[0, 0] / (groups * group), query_grads)


def solution(mesh):
    placed = (
        P(("query", "passage"), None, None),
        P("passage", None, None),
        P(),
        P("query", None, None),
        P("query", None),
        P("query", None),
    )
    return jax.shard_map(
        body,
        mesh=mesh,
        in_specs=placed,
        out_specs=(P(), P(("query", "passage"), None, None)),
        check_vma=False,
    )
```

```python
import math
import jax
import jax.numpy as jnp
from jax import lax
from jax.experimental import pallas as pl
from jax.experimental.pallas import tpu as pltpu
from jax.sharding import PartitionSpec as P

LANES = 128
SLOTS = 4
AHEAD = 16
UNROLL = 8
UNITS = 176
PLEN = 128
PADDED = 256
TOLD = 4
FLOOR = -1e30
NT = (((1,), (1,)), ((), ()))
VMEM = pl.BlockSpec(memory_space=pltpu.VMEM)
HBM = pl.BlockSpec(memory_space=pltpu.HBM)
SMEM = pl.BlockSpec(memory_space=pltpu.SMEM)
f32 = jnp.float32
bf16 = jnp.bfloat16
i32 = jnp.int32


def held(shape, dtype):
    return pltpu.VMEM(shape, dtype)


def in_hbm(array):
    return pltpu.with_memory_space_constraint(array, pltpu.HBM)


def call(kernel, outs, in_specs, cost, scratch=()):
    return pl.pallas_call(
        kernel,
        out_shape=outs,
        in_specs=in_specs,
        out_specs=tuple(HBM if getattr(o, "memory_space", None) == pltpu.HBM else VMEM for o in outs),
        scratch_shapes=scratch,
        compiler_params=pltpu.CompilerParams(vmem_limit_bytes=24 * 1024 * 1024),
        cost_estimate=pl.CostEstimate(flops=cost, bytes_accessed=cost // 100, transcendentals=0),
    )


def turns(shards):
    rows = shards // 4
    return [4 * (3 * row % rows) + column for column in range(4) for row in range(rows)]


def iota(shape, axis):
    return lax.broadcasted_iota(i32, shape, axis)


def plan(shard_ref, local_ref, teacher_ref, lengths_ref, table_ref, slot_ref, count_ref, mass_ref, share_ref, entropy_ref):
    group, passages = shard_ref.shape[0], lengths_ref.shape[1]
    units, padded = count_ref.shape[0], PADDED
    teacher = teacher_ref[...]
    top = jnp.max(teacher, axis=1, keepdims=True)
    log_teacher = teacher - (top + jnp.log(jnp.sum(jnp.exp(teacher - top), axis=1, keepdims=True)))
    probs = jnp.exp(log_teacher)
    here = shard_ref[...] == lax.axis_index("passage")
    entropy_ref[...] = jnp.broadcast_to(jnp.sum(jnp.where(here, probs * log_teacher, 0.0), keepdims=True), entropy_ref.shape)
    key = jnp.where(here, local_ref[...], -1)
    row = iota((passages, key.shape[1]), 0)
    lane = iota((passages, LANES), 1)
    count = jnp.zeros((passages, LANES), f32)
    mass = jnp.zeros((passages, LANES), f32)
    for q in range(group):
        hit = key[q : q + 1, :] == row
        count = jnp.where(lane == q, jnp.sum(jnp.where(hit, 1.0, 0.0), axis=1, keepdims=True), count)
        mass = jnp.where(lane == q, jnp.sum(jnp.where(hit, probs[q : q + 1, :], 0.0), axis=1, keepdims=True), mass)
    live = count > 0.0
    live_b = jnp.where(live, 1.0, 0.0).astype(bf16)
    before = jnp.where(iota((LANES, LANES), 0) < iota((LANES, LANES), 1), 1.0, 0.0).astype(bf16)
    rank = jnp.dot(live_b, before, preferred_element_type=f32)
    rank = jnp.where(live, rank, -1.0)
    named = lax.dot_general(jnp.ones((8, LANES), bf16), live_b, NT, preferred_element_type=f32)
    needed = ((named.astype(i32) + (SLOTS - 1)) // SLOTS).astype(f32)
    before_p = jnp.where(iota((passages, passages), 0) < iota((passages, passages), 1), 1.0, 0.0).astype(bf16)
    first = jnp.dot(needed.astype(bf16), before_p, preferred_element_type=f32)
    needed, first = needed[0:1, :], first[0:1, :]
    total = jnp.sum(needed, axis=1, keepdims=True)
    unit = iota((padded, passages), 0).astype(f32)
    own = (unit >= first) & (unit < first + needed)
    own_f = jnp.where(own, 1.0, 0.0)
    own_b = own_f.astype(bf16)
    passage = jnp.sum(jnp.where(own, iota((padded, passages), 1).astype(f32), 0.0), axis=1, keepdims=True)
    length = jnp.sum(jnp.where(own, lengths_ref[...].astype(f32), 0.0), axis=1, keepdims=True)
    offset = jnp.sum(jnp.where(own, unit - first, 0.0), axis=1, keepdims=True) * SLOTS
    wide = iota((padded, LANES), 1)
    used = iota((padded, LANES), 0).astype(f32) < total
    unit_rank = jnp.dot(own_b, rank.astype(bf16), preferred_element_type=f32)
    slot = jnp.where(used & (unit_rank >= 0.0), unit_rank - offset, -1.0)
    here = (slot >= 0.0) & (slot < float(SLOTS))
    slot = jnp.where(here, slot, -1.0)
    unit_count = jnp.where(here, jnp.dot(own_b, count.astype(bf16), preferred_element_type=f32), 0.0)
    unit_mass = jnp.dot(own_f, mass, preferred_element_type=f32, precision=lax.Precision.HIGHEST)
    unit_mass = jnp.where(here, unit_mass, 0.0)
    slot_ref[...] = slot[:units]
    count_ref[...] = unit_count[:units]
    mass_ref[...] = unit_mass[:units]
    ints = jnp.where(wide == SLOTS, passage, 0.0)
    eights = jnp.floor(length * 0.125) * 8.0
    ints = jnp.where(wide == SLOTS + 1, PLEN - eights, ints)
    ints = jnp.where(wide == SLOTS + 3, length - eights, ints)
    ints = jnp.where(wide == SLOTS + 2, total, ints)
    wide_f = wide.astype(f32)
    shares = jnp.zeros((units, LANES), f32)
    for k in range(SLOTS):
        pick = slot == float(k)
        query = group + jnp.sum(jnp.where(pick, wide_f - group, 0.0), axis=1, keepdims=True)
        ints = jnp.where(wide == k, query, ints)
        share = jnp.sum(jnp.where(pick, unit_mass, 0.0)[:units], axis=1, keepdims=True)
        shares = jnp.where(wide[:units] == SLOTS + k, share, shares)
    share_ref[...] = shares
    ints = jnp.transpose(ints).astype(i32)
    for k in range(SLOTS + 4):
        for half in range(padded // LANES):
            table_ref[pl.ds(k * (padded // LANES) + half, 1), :] = ints[k : k + 1, half * LANES : (half + 1) * LANES]


def field(k):
    return k * PADDED


def trips(table_ref, size):
    return (table_ref[field(SLOTS + 2)] + (size - 1)) // size


def score(
    table_ref, query_ref, passage_ref, slot_ref, count_ref, mass_ref, share_ref, entropy_ref,
    weight_ref, factor_ref, local_ref, own_ref,
    double_ref, row_ref, logits_ref, buffer_ref, scale_ref, cap_ref, turned_ref, sems,
):
    group, qlen = query_ref.shape[0], query_ref.shape[1]
    units, columns, plen = weight_ref.shape
    double_ref[:group] = query_ref[...] * 2
    double_ref[group] = jnp.zeros(double_ref.shape[1:], bf16)
    row_ref[...] = jnp.zeros(row_ref.shape, f32)
    for part in range(8):
        cap_ref[part] = jnp.where(iota((2 * plen, columns), 0) < plen + part, -FLOOR, FLOOR)
    rounds = trips(table_ref, AHEAD)

    def out(t):
        first = pl.multiple_of(t * AHEAD, AHEAD)
        return pltpu.make_async_copy(
            buffer_ref.at[pl.ds(first + AHEAD, AHEAD)], weight_ref.at[pl.ds(first, AHEAD)], sems.at[t]
        )

    def turn(u):
        tokens = [double_ref[table_ref[field(k) + u]] for k in range(SLOTS)]
        return jnp.transpose(jnp.concatenate(tokens, axis=0))

    for j in range(AHEAD):
        turned_ref[j] = turn(j)

    def some(t, carry):
        for j in range(AHEAD):
            u = t * AHEAD + j
            old = logits_ref[j]
            p = table_ref[field(SLOTS) + u]
            tokens = turned_ref[j]
            turned_ref[j] = turn(u + AHEAD)
            logits = jnp.dot(passage_ref[p], tokens, preferred_element_type=f32)
            start = pl.multiple_of(table_ref[field(SLOTS + 1) + u], 8)
            logits_ref[j] = jnp.minimum(logits, cap_ref[table_ref[field(SLOTS + 3) + u], pl.ds(start, plen), :])
            top = jnp.max(old, axis=0, keepdims=True)
            terms = jnp.exp(old - top)
            total = jnp.sum(terms, axis=0, keepdims=True)
            buffer_ref[u] = jnp.transpose((terms * (1.0 / total)).astype(bf16))
            row_ref[pl.ds(u, 1), :] = top + jnp.log(total)

        @pl.when(t > 0)
        def _():
            out(t - 1).start()

        return carry

    lax.fori_loop(0, rounds + 1, some, 0)
    same = iota((columns, LANES), 0) // qlen == iota((columns, LANES), 1)
    rows = row_ref[pl.ds(AHEAD, units), :]
    halves = jnp.where(same, 0.5, 0.0).astype(bf16)
    summed = jnp.zeros((units, LANES), f32)
    for _ in range(3):
        part = rows.astype(bf16)
        summed += jnp.dot(part, halves, preferred_element_type=f32)
        rows -= part.astype(f32)
    slot, count, mass = slot_ref[...], count_ref[...], mass_ref[...]
    scores = jnp.zeros((units, LANES), f32)
    for k in range(SLOTS):
        scores = jnp.where(slot == float(k), jnp.broadcast_to(summed[:, k : k + 1], (units, LANES)), scores)
    live = slot >= 0.0
    top = jnp.max(jnp.where(live, scores, FLOOR), axis=0, keepdims=True)
    gap = jnp.where(live, scores - top, 0.0)
    student = jnp.where(live, count * jnp.exp(gap), 0.0)
    scale = share_ref[...]
    wide = iota((units, LANES), 1)
    for k in range(SLOTS):
        scale = jnp.where(wide == k, jnp.sum(jnp.where(slot == float(k), student, 0.0), axis=1, keepdims=True), scale)
    scale_ref[...] = scale
    factors = pltpu.make_async_copy(scale_ref, factor_ref, sems.at[units // AHEAD])
    factors.start()
    total = jnp.sum(student, axis=0, keepdims=True)
    lane = iota((1, LANES), 1)
    cross = jnp.sum(mass * gap, axis=0, keepdims=True) - jnp.where(lane == 0, entropy_ref[...], 0.0)
    kept = jnp.sum(mass, axis=0, keepdims=True)
    packed = jnp.where(lane < group, top, 0.0)
    for k, part in enumerate((total, cross, kept)):
        moved = pltpu.roll(jnp.broadcast_to(part, (8, LANES)), (k + 1) * group, 1)[0:1]
        packed = jnp.where(lane // group == k + 1, moved, packed)
    local_ref[...] = jnp.broadcast_to(packed, local_ref.shape)
    own_ref[...] = jnp.broadcast_to(packed, own_ref.shape)

    def finish(t, carry):
        out(t).wait()
        return carry

    lax.fori_loop(0, rounds, finish, 0)
    factors.wait()


def terms_of(table_ref, weight_ref, passage_ref, factor_ref, sums_ref, scale_ref, spread_ref, grads_ref, buffer_ref, sems):
    qlen = sums_ref.shape[1] // 2
    units = weight_ref.shape[0]
    rounds = trips(table_ref, UNROLL)
    factors = pltpu.make_async_copy(factor_ref, scale_ref, sems.at[units // UNROLL])
    factors.start()

    def into(t):
        part = pl.ds(pl.multiple_of(t * UNROLL, UNROLL), UNROLL)
        return pltpu.make_async_copy(weight_ref.at[part], buffer_ref.at[part], sems.at[t])

    def begin(t, carry):
        into(t).start()
        return carry

    lax.fori_loop(0, rounds, begin, 0)
    sums_ref[...] = jnp.zeros(sums_ref.shape, f32)
    grads_ref[...] = jnp.zeros(grads_ref.shape, f32)
    factors.wait()
    scale = scale_ref[...]
    for k in range(2 * SLOTS):
        spread_ref[k] = jnp.broadcast_to(scale[:, k : k + 1], scale.shape)

    def some(t, carry):
        @pl.when(t < rounds)
        def _():
            into(t).wait()

        for j in range(UNROLL):
            old = grads_ref[j]
            late = jnp.minimum(t, rounds - 1) * UNROLL + j
            grads_ref[j] = jnp.dot(buffer_ref[late], passage_ref[table_ref[field(SLOTS) + late]], preferred_element_type=f32)
            u = jnp.maximum(t - 1, 0) * UNROLL + j
            queries = [table_ref[field(k) + u] for k in range(SLOTS)]
            sums = [sums_ref[q] for q in queries]
            for k, q in enumerate(queries):
                part = old[k * qlen : (k + 1) * qlen]
                student, share = spread_ref[k, pl.ds(u, 1), :], spread_ref[SLOTS + k, pl.ds(u, 1), :]
                sums_ref[q] = sums[k] + jnp.concatenate([student * part, share * part], axis=0)
        return carry

    @pl.when(rounds > 0)
    def _():
        lax.fori_loop(0, rounds + 1, some, 0)


def shared(parts):
    group = LANES // 4
    total, cross, kept = (pltpu.roll(parts, LANES - (k + 1) * group, 1) for k in range(3))
    top = jnp.max(parts, axis=0, keepdims=True)
    lse = top + jnp.log(jnp.sum(total * jnp.exp(parts - top), axis=0, keepdims=True))
    return lse, cross, kept


def join(parts_ref, own_ref, sums_ref, grads_ref, loss_ref):
    group, qlen = grads_ref.shape[0], grads_ref.shape[1]
    shards = parts_ref.shape[0] // TOLD
    mine = lax.axis_index("query") % TOLD
    lane = iota((1, LANES), 1)
    loss = jnp.zeros((1, 1), f32)
    lse = jnp.zeros((1, LANES), f32)
    for side in range(TOLD):
        parts = parts_ref[side * shards : (side + 1) * shards]
        found, cross, kept = shared(parts)
        agreed = jnp.sum(cross + kept * (parts - found), axis=0, keepdims=True)
        loss = loss - jnp.sum(jnp.where(lane < group, agreed, 0.0), axis=1, keepdims=True)
        lse = jnp.where(mine == side, found, lse)
    loss_ref[...] = jnp.broadcast_to(loss, loss_ref.shape)
    factor = jnp.where(lane < group, jnp.exp(own_ref[0:1, :] - lse), 0.0)
    factors = jnp.transpose(jnp.broadcast_to(factor, (LANES, LANES)))
    for place, q in enumerate(turns(group)):
        grads_ref[place] = sums_ref[q, :qlen] * factors[q : q + 1, :] - sums_ref[q, qlen:]


def body(query_tokens, passage_tokens, passage_lengths, cand_shard, cand_local, teacher_scores):
    shards, groups = lax.axis_size("passage"), lax.axis_size("query")
    me = lax.axis_index("passage")
    group, cands = cand_local.shape
    qlen, dim = query_tokens.shape[1:]
    passages, plen, _ = passage_tokens.shape
    units = UNITS
    queries = lax.all_to_all(jnp.broadcast_to(query_tokens, (shards, qlen, dim)), "passage", 0, 0, tiled=True)
    lengths = lax.dynamic_slice_in_dim(passage_lengths, me * passages, passages).reshape(1, passages)
    table, slot, count, mass, share, entropy = call(
        plan,
        (
            held((2 * SLOTS * PADDED // LANES, LANES), i32),
            held((units, LANES), f32),
            held((units, LANES), f32),
            held((units, LANES), f32),
            held((units, LANES), f32),
            held((1, LANES), f32),
        ),
        [VMEM, VMEM, VMEM, VMEM],
        int(2e9),
    )(cand_shard.reshape(group, cands), cand_local, teacher_scores, lengths)
    weights, factors, local, own = call(
        score,
        (
            pltpu.HBM((units, SLOTS * qlen, plen), bf16),
            pltpu.HBM((units, LANES), f32),
            held((TOLD * shards, LANES), f32),
            held((8, LANES), f32),
        ),
        [SMEM, VMEM, VMEM, VMEM, VMEM, VMEM, VMEM, VMEM],
        int(4e9),
        [
            pltpu.VMEM((group + 1, qlen, dim), bf16),
            pltpu.VMEM((AHEAD + units, LANES), f32),
            pltpu.VMEM((AHEAD, plen, SLOTS * qlen), f32),
            pltpu.VMEM((AHEAD + units, SLOTS * qlen, plen), bf16),
            pltpu.VMEM((units, LANES), f32),
            pltpu.VMEM((8, 2 * plen, SLOTS * qlen), f32),
            pltpu.VMEM((AHEAD, dim, SLOTS * qlen), bf16),
            pltpu.SemaphoreType.DMA((units // AHEAD + 1,)),
        ],
    )(table.reshape(-1), queries, passage_tokens, slot, count, mass, share, entropy)
    told = [list(range(a, a + TOLD)) for a in range(0, groups, TOLD)]
    sets = [[g * shards + s for g in members for s in range(shards)] for members in told]
    parts = lax.all_to_all(
        local.reshape(TOLD * shards, 1, LANES), ("query", "passage"), 0, 0, tiled=True, axis_index_groups=sets
    )
    (sums,) = call(
        terms_of,
        (held((group + 1, 2 * qlen, dim), f32),),
        [SMEM, HBM, VMEM, HBM],
        int(4e9),
        [
            pltpu.VMEM((units, LANES), f32),
            pltpu.VMEM((2 * SLOTS, units, LANES), f32),
            pltpu.VMEM((UNROLL, SLOTS * qlen, dim), f32),
            pltpu.VMEM((units, SLOTS * qlen, plen), bf16),
            pltpu.SemaphoreType.DMA((units // UNROLL + 1,)),
        ],
    )(table.reshape(-1), in_hbm(weights), passage_tokens, in_hbm(factors))
    parts = parts.reshape(TOLD * shards, LANES)
    grads, loss = call(
        join,
        (jax.ShapeDtypeStruct((group, qlen, dim), f32), jax.ShapeDtypeStruct((1, LANES), f32)),
        [VMEM, VMEM, VMEM],
        int(1e9),
    )(parts, own, sums)
    sent = lax.all_to_all(grads, "passage", 0, 0, tiled=True, axis_index_groups=[turns(shards)])
    left = [list(members) for members in zip(*told)]
    loss = jnp.sum(lax.all_gather(loss, "query", axis=0, tiled=True, axis_index_groups=left), axis=0, keepdims=True)
    query_grads = jnp.sum(sent, axis=0, keepdims=True)
    return (loss[0, 0] / (groups * group), query_grads)


def solution(mesh):
    placed = (
        P(("query", "passage"), None, None),
        P("passage", None, None),
        P(),
        P("query", None, None),
        P("query", None),
        P("query", None),
    )
    return jax.shard_map(
        body,
        mesh=mesh,
        in_specs=placed,
        out_specs=(P(), P(("query", "passage"), None, None)),
        check_vma=False,
    )
```
